768 devices in a mesh: seq: 384 (over z, x, y), head: 2 (over core).
Axes of the slice: x: 4, y: 8, z: 12, core: 2. Of those that a mesh axis runs over, the one named last changes fastest.
Arguments:
- query_raw: bfloat16 [98304, 8, 128], P('seq', 'head'), may hold values from -6 to 6
- key_raw: bfloat16 [98304, 8, 128], P('seq', 'head'), may hold values from -6 to 6
- value_raw: bfloat16 [98304, 8, 128], P('seq', 'head'), may hold values from -6 to 6
- out_gain: float32 [8, 128], P('head'), may hold values from 0.5 to 1.5
- out_grad: bfloat16 [98304, 8, 128], P('seq', 'head'), may hold values from -6 to 6
Outputs:
- normed_out: bfloat16 [98304, 8, 128], P('seq', 'head')
- query_grad: bfloat16 [98304, 8, 128], P('seq', 'head')
- key_grad: bfloat16 [98304, 8, 128], P('seq', 'head')
- value_grad: bfloat16 [98304, 8, 128], P('seq', 'head')
The draws below stay inside these ranges and needn't reach their ends.
All inputs are finite; a program needn't handle non-finite values.
Results may differ from the reference program's by a relative error of at most 0.0065.
Values sent between devices are 32-bit elements; how exact they have to be, the bound alone decides.
A program may use at most 32 MiB of HBM per device.

```python
import jax
import jax.numpy as jnp
from jax import lax

DH = 128
GROUP = 256
TOKENS = 98304
HEADS = 8


def block_scale(rng, shape, cuts, smallest, high):
    level = 1.0
    for axis_at, parts in cuts:
        steps = jax.random.uniform(jax.random.fold_in(jax.random.fold_in(rng, 6), axis_at), (parts,), jnp.float32, smallest / len(cuts), high / len(cuts))
        level = level * jnp.repeat(jnp.exp(steps), shape[axis_at] // parts).reshape((-1,) + (1,) * (len(shape) - 1 - axis_at))
    return level


def centred(rng, shape, scale, limit, shards=(), kind=jnp.bfloat16):
    drawn = jax.random.normal(rng, shape, jnp.float32) * scale
    if len(shards) > 0:
        drawn = block_scale(rng, shape, shards, -0.22, 0.18) * drawn
    return jnp.clip(drawn, min=-limit, max=limit).astype(kind)


def setup_inputs(seed: int = 0) -> dict:
    streams_of = jax.random.split(jax.random.key(seed), 6)
    return {
        "query_raw": centred(streams_of[0], (TOKENS, HEADS, DH), 1.0, 6.0, ((0, 384), (1, 2))),
        "key_raw": centred(streams_of[1], (TOKENS, HEADS, DH), 1.0, 6.0, ((0, 384), (1, 2))),
        "value_raw": centred(streams_of[2], (TOKENS, HEADS, DH), 1.0, 6.0, ((0, 384), (1, 2))),
        "out_gain": jnp.clip(1.0 + 0.1 * jax.random.normal(streams_of[3], (HEADS, DH), jnp.float32), 0.5, 1.5),
        "out_grad": centred(streams_of[4], (TOKENS, HEADS, DH), 1.0, 6.0, ((0, 384), (1, 2))),
    }


def silu_grad(raw):
    sigma = jax.nn.sigmoid(raw)
    return sigma * (1.0 + raw * (1.0 - sigma))

def causal_mask(length):
    rows = lax.broadcasted_iota(jnp.int32, (length, length), 0)
    cols = lax.broadcasted_iota(jnp.int32, (length, length), 1)
    return cols <= rows

def round_trip(value):
    return lax.optimization_barrier(value.astype(jnp.bfloat16)).astype(jnp.float32)

def reference(query_raw, key_raw, value_raw, out_gain, out_grad):
    blocks = TOKENS // GROUP
    blocked = (blocks, GROUP, HEADS, DH)
    query_act = jax.nn.silu(query_raw.astype(jnp.float32)).astype(jnp.bfloat16)
    key_act = jax.nn.silu(key_raw.astype(jnp.float32)).astype(jnp.bfloat16)
    query_blk = query_act.reshape(blocked)
    key_blk = key_act.reshape(blocked)
    value_blk = value_raw.reshape(blocked)
    grad_blk = out_grad.reshape(blocked)
    mask = causal_mask(GROUP)
    features = HEADS * DH
    gain_f = out_gain.astype(jnp.float32)

    def forward_step(state, block):
        query_c, key_c, value_c, grad_c = block
        query_f = query_c.astype(jnp.float32)
        key_f = key_c.astype(jnp.float32)
        value_f = value_c.astype(jnp.float32)
        scores = jnp.einsum('thd,shd->hts', query_f, key_f)
        attn = round_trip(jnp.where(mask[None], scores, 0.0))
        state_b = round_trip(state)
        mixed = jnp.einsum('hts,she->the', attn, value_f) + jnp.einsum('thd,hde->the', query_f, state_b)
        grad_in = grad_c.astype(jnp.float32) * gain_f
        sq_total = lax.optimization_barrier(jnp.sum(mixed * mixed, axis=(1, 2)))
        cross_total = lax.optimization_barrier(jnp.sum(grad_in * mixed, axis=(1, 2)))
        inv_rms = lax.rsqrt(sq_total / features + 1e-06)
        normed = (mixed * inv_rms[:, None, None] * gain_f).astype(jnp.bfloat16)
        delta = (grad_in * inv_rms[:, None, None] - mixed * (cross_total * inv_rms ** 3 / features)[:, None, None]).astype(jnp.bfloat16)
        state = state + jnp.einsum('shd,she->hde', key_f, value_f)
        return (state, (normed, delta, state_b.astype(jnp.bfloat16)))
    start = jnp.zeros((HEADS, DH, DH), jnp.float32)
    unused, (normed, delta, states) = lax.scan(forward_step, start, (query_blk, key_blk, value_blk, grad_blk))
    query_raw_blk = query_raw.reshape(blocked)
    key_raw_blk = key_raw.reshape(blocked)

    def backward_step(grad_state, block):
        query_c, key_c, value_c, delta_c, state_c, qraw_c, kraw_c = block
        query_f = query_c.astype(jnp.float32)
        key_f = key_c.astype(jnp.float32)
        value_f = value_c.astype(jnp.float32)
        delta_f = delta_c.astype(jnp.float32)
        state_f = state_c.astype(jnp.float32)
        grad_b = round_trip(grad_state)
        scores = jnp.einsum('thd,shd->hts', query_f, key_f)
        attn = round_trip(jnp.where(mask[None], scores, 0.0))
        bscore = round_trip(jnp.where(mask[None], jnp.einsum('the,she->hts', delta_f, value_f), 0.0))
        dquery = jnp.einsum('hts,shd->thd', bscore, key_f) + jnp.einsum('the,hde->thd', delta_f, state_f)
        dkey = jnp.einsum('hts,thd->shd', bscore, query_f) + jnp.einsum('she,hde->shd', value_f, grad_b)
        dvalue = jnp.einsum('hts,the->she', attn, delta_f) + jnp.einsum('shd,hde->she', key_f, grad_b)
        query_out = (dquery * silu_grad(qraw_c.astype(jnp.float32))).astype(jnp.bfloat16)
        key_out = (dkey * silu_grad(kraw_c.astype(jnp.float32))).astype(jnp.bfloat16)
        grad_state = grad_state + jnp.einsum('thd,the->hde', query_f, delta_f)
        return (grad_state, (query_out, key_out, dvalue.astype(jnp.bfloat16)))
    unused_two, (query_grad, key_grad, value_grad) = lax.scan(backward_step, start, (query_blk, key_blk, value_blk, delta, states, query_raw_blk, key_raw_blk), reverse=True)
    whole = (TOKENS, HEADS, DH)
    return (normed.reshape(whole), query_grad.reshape(whole), key_grad.reshape(whole), value_grad.reshape(whole))
```

```python
import functools

import jax
import jax.numpy as jnp
from jax import lax
from jax.experimental import pallas as pl
from jax.experimental.pallas import tpu as pltpu
from jax.sharding import PartitionSpec as P

GROUP = 256
DH = 128
PLANE = 32
CHUNKS = 1
MESH = pl.DeviceIdType.MESH
F32 = jnp.float32
BF16 = jnp.bfloat16


def dot(lhs, rhs, contract):
    return lax.dot_general(lhs, rhs, (contract, ((), ())), preferred_element_type=F32)


def nn(lhs, rhs):
    return dot(lhs, rhs, ((1,), (0,)))


def nt(lhs, rhs):
    return dot(lhs, rhs, ((1,), (1,)))


def tn(lhs, rhs):
    return dot(lhs, rhs, ((0,), (0,)))


def kernel(
    levels,
    heads,
    cores,
    q_hbm,
    k_hbm,
    v_hbm,
    gain_ref,
    g_hbm,
    normed_hbm,
    qg_hbm,
    kg_hbm,
    vg_hbm,
    raw,
    out_buf,
    qact,
    kact,
    vact,
    qslope,
    kslope,
    grad_in,
    attn,
    mixed,
    delta,
    dk,
    dv,
    state_b,
    own,
    gathered,
    prefix,
    total,
    z_slots,
    state,
    stats,
    in_sem,
    out_sem,
    send_sem,
    recv_sem,
    z_send_sem,
    z_recv_sem,
    stat_sem,
):
    seq = lax.axis_index("seq")
    core = lax.axis_index("head")
    level = seq // PLANE
    place = lax.rem(seq, PLANE)
    rows = heads * DH // (CHUNKS * PLANE)
    span = heads * DH // CHUNKS
    per = heads // CHUNKS
    width = GROUP // heads

    def plane_peer(step):
        return lax.rem(place + step, PLANE)

    barrier = pltpu.get_barrier_semaphore()

    def greet_plane(step, carry):
        pl.semaphore_signal(
            barrier, inc=1, device_id=(level * PLANE + plane_peer(step), core), device_id_type=MESH
        )
        return carry

    def greet_level(step, carry):
        other = lax.rem(level + step, levels)
        pl.semaphore_signal(
            barrier, inc=1, device_id=(other * PLANE + place, core), device_id_type=MESH
        )
        return carry

    loads = [
        pltpu.make_async_copy(hbm, raw.at[i], in_sem.at[i])
        for i, hbm in enumerate((k_hbm, v_hbm, q_hbm, g_hbm))
    ]
    for load in loads:
        load.start()
    lax.fori_loop(1, PLANE, greet_plane, 0)
    lax.fori_loop(1, levels, greet_level, 0)
    pl.semaphore_signal(barrier, inc=1, device_id=(seq, 1 - core), device_id_type=MESH)

    row = lax.broadcasted_iota(jnp.int32, (GROUP, GROUP), 0)
    col = lax.broadcasted_iota(jnp.int32, (GROUP, GROUP), 1)
    causal = col <= row
    sort = jnp.where(col == lax.rem(row, width) * heads + row // width, 1.0, 0.0).astype(BF16)
    unsort = jnp.where(col == lax.rem(row, heads) * width + row // heads, 1.0, 0.0).astype(BF16)

    def sorted_tiles(i):
        for tile in range(heads):
            yield tile, nn(sort, raw[i, pl.ds(tile * GROUP, GROUP), :])

    def put(dst, tile, value):
        for h in range(heads):
            dst[h, pl.ds(tile * width, width), :] = value[h * width : (h + 1) * width].astype(
                dst.dtype
            )

    def activate(i, act, slope):
        for tile, value in sorted_tiles(i):
            sigma = jax.nn.sigmoid(value)
            put(act, tile, value * sigma)
            put(slope, tile, sigma * (1.0 + value * (1.0 - sigma)))

    def store(i, hbm, head_value):
        values = [head_value(h).astype(BF16) for h in range(heads)]
        for tile in range(heads):
            piece = jnp.concatenate(
                [value[tile * width : (tile + 1) * width] for value in values], axis=0
            )
            out_buf[i, pl.ds(tile * GROUP, GROUP), :] = nn(unsort, piece).astype(BF16)
        copy = pltpu.make_async_copy(out_buf.at[i], hbm, out_sem.at[i])
        copy.start()
        return copy

    def bytes_of(ref, sem):
        return pltpu.make_async_copy(ref, ref, sem)

    others = pl.ds(0, PLANE - 1)

    def scatter(scan, chunk):
        def send(step, carry):
            peer = plane_peer(step)
            pltpu.make_async_remote_copy(
                src_ref=own.at[scan, pl.ds(chunk * span + peer * rows, rows), :],
                dst_ref=gathered.at[scan, chunk, place],
                send_sem=send_sem.at[scan, 0, chunk],
                recv_sem=recv_sem.at[scan, 0, chunk],
                device_id=(level * PLANE + peer, core),
                device_id_type=MESH,
            ).start()
            return carry

        lax.fori_loop(1, PLANE, send, 0)
        gathered[scan, chunk, place] = own[scan, pl.ds(chunk * span + place * rows, rows), :]

    def wait_scatter(scan, chunk):
        bytes_of(gathered.at[scan, chunk, others], recv_sem.at[scan, 0, chunk]).wait()

    def wait_scatter_send(scan, chunk):
        bytes_of(gathered.at[scan, chunk, others], send_sem.at[scan, 0, chunk]).wait()

    def follows(scan, step):
        other = level + step if scan == 0 else level - step
        return (other < levels) if scan == 0 else (other >= 0), other

    def z_copy(scan, chunk, target):
        return pltpu.make_async_remote_copy(
            src_ref=total.at[scan, chunk],
            dst_ref=z_slots.at[scan, chunk, level],
            send_sem=z_send_sem.at[scan, chunk, target],
            recv_sem=z_recv_sem.at[scan, chunk, level],
            device_id=(target * PLANE + place, core),
            device_id_type=MESH,
        )

    def own_prefix(scan, chunk):
        acc = jnp.zeros((rows, DH), F32)
        order = range(PLANE) if scan == 0 else range(PLANE - 1, -1, -1)
        for p in order:
            prefix[scan, chunk, p] = acc
            acc = acc + gathered[scan, chunk, p]
        total[scan, chunk] = acc
        for step in range(1, levels):
            needed, other = follows(scan, step)

            @pl.when(needed)
            def _():
                z_copy(scan, chunk, other).start()

    def level_prefix(scan, chunk):
        z_slots[scan, chunk, level] = jnp.zeros((rows, DH), F32)
        for source in range(levels):
            earlier = source < level if scan == 0 else source > level

            @pl.when(earlier)
            def _():
                bytes_of(
                    z_slots.at[scan, chunk, source], z_recv_sem.at[scan, chunk, source]
                ).wait()

            @pl.when(jnp.logical_not(earlier))
            def _():
                z_slots[scan, chunk, source] = jnp.zeros((rows, DH), F32)

        acc = jnp.zeros((rows, DH), F32)
        for source in range(levels):
            acc = acc + z_slots[scan, chunk, source]
        for p in range(PLANE):
            prefix[scan, chunk, p] = prefix[scan, chunk, p] + acc

    def give_back(scan, chunk):
        def send(step, carry):
            peer = plane_peer(step)
            pltpu.make_async_remote_copy(
                src_ref=prefix.at[scan, chunk, peer],
                dst_ref=state.at[scan, chunk, place],
                send_sem=send_sem.at[scan, 1, chunk],
                recv_sem=recv_sem.at[scan, 1, chunk],
                device_id=(level * PLANE + peer, core),
                device_id_type=MESH,
            ).start()
            return carry

        lax.fori_loop(1, PLANE, send, 0)
        state[scan, chunk, place] = prefix[scan, chunk, place]

    def wait_back(scan, chunk):
        bytes_of(state.at[scan, chunk, others], recv_sem.at[scan, 1, chunk]).wait()

    def drain(scan):
        for chunk in range(CHUNKS):
            wait_scatter_send(scan, chunk)
            bytes_of(state.at[scan, chunk, others], send_sem.at[scan, 1, chunk]).wait()
            for step in range(1, levels):
                needed, other = follows(scan, step)

                @pl.when(needed)
                def _():
                    z_copy(scan, chunk, other).wait_send()

    def middle(scan):
        for chunk in range(CHUNKS):
            wait_scatter(scan, chunk)
            own_prefix(scan, chunk)
        for chunk in range(CHUNKS):
            level_prefix(scan, chunk)
            give_back(scan, chunk)

    def scanned(scan, h):
        chunk, at = h // per, h % per
        parts = PLANE // per
        return state[scan, chunk, pl.ds(at * parts, parts)].reshape(DH, DH).astype(BF16)

    loads[0].wait()
    activate(0, kact, kslope)
    loads[1].wait()
    for tile, value in sorted_tiles(1):
        put(vact, tile, value)
    for h in range(heads):
        own[0, pl.ds(h * DH, DH), :] = tn(kact[h], vact[h])

    pl.semaphore_wait(barrier, PLANE - 1 + levels - 1 + 1)
    for chunk in range(CHUNKS):
        scatter(0, chunk)

    loads[2].wait()
    activate(2, qact, qslope)
    loads[3].wait()
    for tile, value in sorted_tiles(3):
        for h in range(heads):
            grad_in[h, pl.ds(tile * width, width), :] = (
                value[h * width : (h + 1) * width] * gain_ref[pl.ds(h, 1), :]
            )
    for h in range(heads):
        scores = nt(qact[h], kact[h])
        attn[h] = jnp.where(causal, scores, 0.0).astype(BF16)
        mixed[h] = nn(attn[h], vact[h])

    middle(0)
    for chunk in range(CHUNKS):
        wait_back(0, chunk)

    square = jnp.zeros((GROUP, DH), F32)
    crossed = jnp.zeros((GROUP, DH), F32)
    for h in range(heads):
        state_b[h] = scanned(0, h)
        value = mixed[h] + nn(qact[h], state_b[h])
        mixed[h] = value
        square = square + value * value
        crossed = crossed + grad_in[h] * value
    square = jnp.sum(square, axis=1, keepdims=True)
    crossed = jnp.sum(crossed, axis=1, keepdims=True)
    lane = lax.broadcasted_iota(jnp.int32, (GROUP, DH), 1)
    stats[0] = jnp.where(lane == 0, square, jnp.where(lane == 1, crossed, 0.0))
    exchange = pltpu.make_async_remote_copy(
        src_ref=stats.at[0],
        dst_ref=stats.at[1],
        send_sem=stat_sem.at[0],
        recv_sem=stat_sem.at[1],
        device_id=(seq, 1 - core),
        device_id_type=MESH,
    )
    exchange.start()
    exchange.wait_recv()
    both = stats[1]
    features = heads * cores * DH
    square = square + both[:, 0:1]
    crossed = crossed + both[:, 1:2]
    inv_rms = lax.rsqrt(square * (1.0 / features) + 1e-06)
    factor = crossed * (inv_rms * inv_rms * inv_rms) * (1.0 / features)
    for h in range(heads):
        delta[h] = (grad_in[h] * inv_rms - mixed[h] * factor).astype(BF16)
        own[1, pl.ds(h * DH, DH), :] = tn(qact[h], delta[h])
        if (h + 1) % per == 0:
            scatter(1, h // per)

    copies = [
        store(0, normed_hbm, lambda h: mixed[h] * inv_rms * gain_ref[pl.ds(h, 1), :])
    ]
    for h in range(heads):
        bscore = jnp.where(causal, nt(delta[h], vact[h]), 0.0).astype(BF16)
        mixed[h] = (nn(bscore, kact[h]) + nt(delta[h], state_b[h])) * qslope[h]
        dk[h] = tn(bscore, qact[h])
        dv[h] = tn(attn[h], delta[h])
    copies.append(store(1, qg_hbm, lambda h: mixed[h]))
    exchange.wait_send()
    drain(0)

    middle(1)
    for chunk in range(CHUNKS):
        wait_back(1, chunk)
    for h in range(heads):
        state_b[h] = scanned(1, h)
    copies.append(store(2, kg_hbm, lambda h: (dk[h] + nt(vact[h], state_b[h])) * kslope[h]))
    copies.append(store(3, vg_hbm, lambda h: dv[h] + nn(kact[h], state_b[h])))
    drain(1)
    for copy in copies:
        copy.wait()


def body(query_raw, key_raw, value_raw, out_gain, out_grad):
    tokens, heads, width = query_raw.shape
    levels = lax.axis_size("seq") // PLANE
    cores = lax.axis_size("head")
    flat = (tokens * heads, width)
    rows = heads * DH // (CHUNKS * PLANE)
    anywhere = pl.BlockSpec(memory_space=pl.ANY)
    in_vmem = pl.BlockSpec(memory_space=pltpu.VMEM)
    per_head = (heads, GROUP, DH)
    dma = pltpu.SemaphoreType.DMA
    outs = pl.pallas_call(
        functools.partial(kernel, levels, heads, cores),
        out_shape=[jax.ShapeDtypeStruct(flat, BF16)] * 4,
        in_specs=[anywhere, anywhere, anywhere, in_vmem, anywhere],
        out_specs=[anywhere] * 4,
        scratch_shapes=[
            pltpu.VMEM((4,) + flat, BF16),
            pltpu.VMEM((4,) + flat, BF16),
            pltpu.VMEM(per_head, BF16),
            pltpu.VMEM(per_head, BF16),
            pltpu.VMEM(per_head, BF16),
            pltpu.VMEM(per_head, F32),
            pltpu.VMEM(per_head, F32),
            pltpu.VMEM(per_head, F32),
            pltpu.VMEM((heads, GROUP, GROUP), BF16),
            pltpu.VMEM(per_head, F32),
            pltpu.VMEM(per_head, BF16),
            pltpu.VMEM(per_head, F32),
            pltpu.VMEM(per_head, F32),
            pltpu.VMEM((heads, DH, DH), BF16),
            pltpu.VMEM((2, heads * DH, DH), F32),
            pltpu.VMEM((2, CHUNKS, PLANE, rows, DH), F32),
            pltpu.VMEM((2, CHUNKS, PLANE, rows, DH), F32),
            pltpu.VMEM((2, CHUNKS, rows, DH), F32),
            pltpu.VMEM((2, CHUNKS, levels, rows, DH), F32),
            pltpu.VMEM((2, CHUNKS, PLANE, rows, DH), F32),
            pltpu.VMEM((2, GROUP, DH), F32),
            dma((4,)),
            dma((4,)),
            dma((2, 2, CHUNKS)),
            dma((2, 2, CHUNKS)),
            dma((2, CHUNKS, levels)),
            dma((2, CHUNKS, levels)),
            dma((2,)),
        ],
        compiler_params=pltpu.CompilerParams(
            collective_id=0, has_side_effects=True, vmem_limit_bytes=60 * 1024 * 1024
        ),
    )(
        query_raw.reshape(flat),
        key_raw.reshape(flat),
        value_raw.reshape(flat),
        out_gain,
        out_grad.reshape(flat),
    )
    return tuple(out.reshape(tokens, heads, width) for out in outs)


def solution(mesh):
    rows = P("seq", "head", None)
    return jax.shard_map(
        body,
        mesh=mesh,
        in_specs=(rows, rows, rows, P("head", None), rows),
        out_specs=(rows,) * 4,
        check_vma=False,
    )
```

```python
import functools

import jax
import jax.numpy as jnp
from jax import lax
from jax.experimental import pallas as pl
from jax.experimental.pallas import tpu as pltpu
from jax.sharding import PartitionSpec as P

GROUP = 256
DH = 128
PLANE = 32
CHUNKS = 2
MESH = pl.DeviceIdType.MESH
F32 = jnp.float32
BF16 = jnp.bfloat16


def dot(lhs, rhs, contract):
    return lax.dot_general(lhs, rhs, (contract, ((), ())), preferred_element_type=F32)


def nn(lhs, rhs):
    return dot(lhs, rhs, ((1,), (0,)))


def nt(lhs, rhs):
    return dot(lhs, rhs, ((1,), (1,)))


def tn(lhs, rhs):
    return dot(lhs, rhs, ((0,), (0,)))


def kernel(
    levels,
    heads,
    cores,
    q_hbm,
    k_hbm,
    v_hbm,
    gain_ref,
    g_hbm,
    normed_out,
    qg_out,
    kg_out,
    vg_out,
    raw,
    qact,
    kact,
    vact,
    qslope,
    kslope,
    grad_in,
    attn,
    mixed,
    delta,
    dk,
    dv,
    state_b,
    own,
    gathered,
    prefix,
    total,
    z_slots,
    state,
    stats,
    in_sem,
    send_sem,
    recv_sem,
    z_send_sem,
    z_recv_sem,
    stat_sem,
):
    seq = lax.axis_index("seq")
    core = lax.axis_index("head")
    level = seq // PLANE
    place = lax.rem(seq, PLANE)
    rows = heads * DH // (CHUNKS * PLANE)
    span = heads * DH // CHUNKS
    per = heads // CHUNKS
    width = GROUP // heads

    def plane_peer(step):
        return lax.rem(place + step, PLANE)

    barrier = pltpu.get_barrier_semaphore()

    def greet_plane(step, carry):
        pl.semaphore_signal(
            barrier, inc=1, device_id=(level * PLANE + plane_peer(step), core), device_id_type=MESH
        )
        return carry

    def greet_level(step, carry):
        other = lax.rem(level + step, levels)
        pl.semaphore_signal(
            barrier, inc=1, device_id=(other * PLANE + place, core), device_id_type=MESH
        )
        return carry

    loads = [
        pltpu.make_async_copy(hbm, raw.at[i], in_sem.at[i])
        for i, hbm in enumerate((k_hbm, v_hbm, q_hbm, g_hbm))
    ]
    for load in loads:
        load.start()
    lax.fori_loop(1, PLANE, greet_plane, 0)
    lax.fori_loop(1, levels, greet_level, 0)
    pl.semaphore_signal(barrier, inc=1, device_id=(seq, 1 - core), device_id_type=MESH)

    row = lax.broadcasted_iota(jnp.int32, (GROUP, GROUP), 0)
    col = lax.broadcasted_iota(jnp.int32, (GROUP, GROUP), 1)
    causal = col <= row
    sort = jnp.where(col == lax.rem(row, width) * heads + row // width, 1.0, 0.0).astype(BF16)
    unsort = jnp.where(col == lax.rem(row, heads) * width + row // heads, 1.0, 0.0).astype(BF16)

    def sorted_tiles(i):
        for tile in range(heads):
            yield tile, nn(sort, raw[i, pl.ds(tile * GROUP, GROUP), :])

    def put(dst, tile, value):
        for h in range(heads):
            dst[h, pl.ds(tile * width, width), :] = value[h * width : (h + 1) * width].astype(
                dst.dtype
            )

    def activate(i, act, slope):
        for tile, value in sorted_tiles(i):
            sigma = jax.nn.sigmoid(value)
            put(act, tile, value * sigma)
            put(slope, tile, sigma * (1.0 + value * (1.0 - sigma)))

    def store(out, head_value):
        values = [head_value(h).astype(BF16) for h in range(heads)]
        for tile in range(heads):
            piece = jnp.concatenate(
                [value[tile * width : (tile + 1) * width] for value in values], axis=0
            )
            out[pl.ds(tile * GROUP, GROUP), :] = nn(unsort, piece).astype(BF16)

    def bytes_of(ref, sem):
        return pltpu.make_async_copy(ref, ref, sem)

    others = pl.ds(0, PLANE - 1)

    def scatter(scan, chunk):
        def send(step, carry):
            peer = plane_peer(step)
            pltpu.make_async_remote_copy(
                src_ref=own.at[scan, pl.ds(chunk * span + peer * rows, rows), :],
                dst_ref=gathered.at[scan, chunk, place],
                send_sem=send_sem.at[scan, 0, chunk],
                recv_sem=recv_sem.at[scan, 0, chunk],
                device_id=(level * PLANE + peer, core),
                device_id_type=MESH,
            ).start()
            return carry

        lax.fori_loop(1, PLANE, send, 0)
        gathered[scan, chunk, place] = own[scan, pl.ds(chunk * span + place * rows, rows), :]

    def wait_scatter(scan, chunk):
        bytes_of(gathered.at[scan, chunk, others], recv_sem.at[scan, 0, chunk]).wait()

    def wait_scatter_send(scan, chunk):
        bytes_of(gathered.at[scan, chunk, others], send_sem.at[scan, 0, chunk]).wait()

    def follows(scan, step):
        other = level + step if scan == 0 else level - step
        return (other < levels) if scan == 0 else (other >= 0), other

    def z_copy(scan, chunk, target):
        return pltpu.make_async_remote_copy(
            src_ref=total.at[scan, chunk],
            dst_ref=z_slots.at[scan, chunk, level],
            send_sem=z_send_sem.at[scan, chunk, target],
            recv_sem=z_recv_sem.at[scan, chunk, level],
            device_id=(target * PLANE + place, core),
            device_id_type=MESH,
        )

    def own_prefix(scan, chunk):
        acc = jnp.zeros((rows, DH), F32)
        order = range(PLANE) if scan == 0 else range(PLANE - 1, -1, -1)
        for p in order:
            prefix[scan, chunk, p] = acc
            acc = acc + gathered[scan, chunk, p]
        total[scan, chunk] = acc
        for step in range(1, levels):
            needed, other = follows(scan, step)

            @pl.when(needed)
            def _():
                z_copy(scan, chunk, other).start()

    def level_prefix(scan, chunk):
        z_slots[scan, chunk, level] = jnp.zeros((rows, DH), F32)
        for source in range(levels):
            earlier = source < level if scan == 0 else source > level

            @pl.when(earlier)
            def _():
                bytes_of(
                    z_slots.at[scan, chunk, source], z_recv_sem.at[scan, chunk, source]
                ).wait()

            @pl.when(jnp.logical_not(earlier))
            def _():
                z_slots[scan, chunk, source] = jnp.zeros((rows, DH), F32)

        acc = jnp.zeros((rows, DH), F32)
        for source in range(levels):
            acc = acc + z_slots[scan, chunk, source]
        for p in range(PLANE):
            prefix[scan, chunk, p] = prefix[scan, chunk, p] + acc

    def give_back(scan, chunk):
        def send(step, carry):
            peer = plane_peer(step)
            pltpu.make_async_remote_copy(
                src_ref=prefix.at[scan, chunk, peer],
                dst_ref=state.at[scan, chunk, place],
                send_sem=send_sem.at[scan, 1, chunk],
                recv_sem=recv_sem.at[scan, 1, chunk],
                device_id=(level * PLANE + peer, core),
                device_id_type=MESH,
            ).start()
            return carry

        lax.fori_loop(1, PLANE, send, 0)
        state[scan, chunk, place] = prefix[scan, chunk, place]

    def wait_back(scan, chunk):
        bytes_of(state.at[scan, chunk, others], recv_sem.at[scan, 1, chunk]).wait()

    def drain(scan):
        for chunk in range(CHUNKS):
            wait_scatter_send(scan, chunk)
            bytes_of(state.at[scan, chunk, others], send_sem.at[scan, 1, chunk]).wait()
            for step in range(1, levels):
                needed, other = follows(scan, step)

                @pl.when(needed)
                def _():
                    z_copy(scan, chunk, other).wait_send()

    def middle(scan, work):
        for chunk in range(CHUNKS):
            wait_scatter(scan, chunk)
            own_prefix(scan, chunk)
        work()
        for chunk in range(CHUNKS):
            level_prefix(scan, chunk)
            give_back(scan, chunk)

    def scanned(scan, h):
        chunk, at = h // per, h % per
        parts = PLANE // per
        return state[scan, chunk, pl.ds(at * parts, parts)].reshape(DH, DH).astype(BF16)

    loads[0].wait()
    activate(0, kact, kslope)
    loads[1].wait()
    for tile, value in sorted_tiles(1):
        put(vact, tile, value)
    for h in range(heads):
        own[0, pl.ds(h * DH, DH), :] = tn(kact[h], vact[h])

    pl.semaphore_wait(barrier, PLANE - 1 + levels - 1 + 1)
    for chunk in range(CHUNKS):
        scatter(0, chunk)

    loads[2].wait()
    activate(2, qact, qslope)
    for h in range(heads):
        scores = nt(qact[h], kact[h])
        attn[h] = jnp.where(causal, scores, 0.0).astype(BF16)
        mixed[h] = nn(attn[h], vact[h])

    def weigh_grad():
        loads[3].wait()
        for tile, value in sorted_tiles(3):
            for h in range(heads):
                grad_in[h, pl.ds(tile * width, width), :] = (
                    value[h * width : (h + 1) * width] * gain_ref[pl.ds(h, 1), :]
                )

    middle(0, weigh_grad)

    square = jnp.zeros((GROUP, DH), F32)
    crossed = jnp.zeros((GROUP, DH), F32)
    for h in range(heads):
        if h % per == 0:
            wait_back(0, h // per)
        state_b[h] = scanned(0, h)
        value = mixed[h] + nn(qact[h], state_b[h])
        mixed[h] = value
        square = square + value * value
        crossed = crossed + grad_in[h] * value
    square = jnp.sum(square, axis=1, keepdims=True)
    crossed = jnp.sum(crossed, axis=1, keepdims=True)
    lane = lax.broadcasted_iota(jnp.int32, (GROUP, DH), 1)
    stats[0] = jnp.where(lane == 0, square, jnp.where(lane == 1, crossed, 0.0))
    exchange = pltpu.make_async_remote_copy(
        src_ref=stats.at[0],
        dst_ref=stats.at[1],
        send_sem=stat_sem.at[0],
        recv_sem=stat_sem.at[1],
        device_id=(seq, 1 - core),
        device_id_type=MESH,
    )
    exchange.start()
    exchange.wait_recv()
    both = stats[1]
    features = heads * cores * DH
    square = square + both[:, 0:1]
    crossed = crossed + both[:, 1:2]
    inv_rms = lax.rsqrt(square * (1.0 / features) + 1e-06)
    factor = crossed * (inv_rms * inv_rms * inv_rms) * (1.0 / features)
    for h in range(heads):
        delta[h] = (grad_in[h] * inv_rms - mixed[h] * factor).astype(BF16)
        own[1, pl.ds(h * DH, DH), :] = tn(qact[h], delta[h])
        if (h + 1) % per == 0:
            scatter(1, h // per)

    store(normed_out, lambda h: mixed[h] * inv_rms * gain_ref[pl.ds(h, 1), :])

    def local_grads(some_heads):
        for h in some_heads:
            bscore = jnp.where(causal, nt(delta[h], vact[h]), 0.0).astype(BF16)
            mixed[h] = (nn(bscore, kact[h]) + nt(delta[h], state_b[h])) * qslope[h]
            dk[h] = tn(bscore, qact[h])
            dv[h] = tn(attn[h], delta[h])

    local_grads(range(heads // 2))
    middle(1, lambda: None)
    local_grads(range(heads // 2, heads))
    store(qg_out, lambda h: mixed[h])
    exchange.wait_send()
    drain(0)

    for h in range(heads):
        if h % per == 0:
            wait_back(1, h // per)
        state_b[h] = scanned(1, h)
        dk[h] = (dk[h] + nt(vact[h], state_b[h])) * kslope[h]
        dv[h] = dv[h] + nn(kact[h], state_b[h])
    store(kg_out, lambda h: dk[h])
    store(vg_out, lambda h: dv[h])
    drain(1)


def deliver(*refs):
    count = len(refs) // 2
    sems = refs[-1]
    copies = [
        pltpu.make_async_copy(refs[i], refs[count + i], sems.at[i]) for i in range(count)
    ]
    for copy in copies:
        copy.start()
    for copy in copies:
        copy.wait()


def body(query_raw, key_raw, value_raw, out_gain, out_grad):
    tokens, heads, width = query_raw.shape
    levels = lax.axis_size("seq") // PLANE
    cores = lax.axis_size("head")
    flat = (tokens * heads, width)
    rows = heads * DH // (CHUNKS * PLANE)
    in_hbm = pl.BlockSpec(memory_space=pltpu.HBM)
    in_vmem = pl.BlockSpec(memory_space=pltpu.VMEM)
    per_head = (heads, GROUP, DH)
    dma = pltpu.SemaphoreType.DMA
    outs = pl.pallas_call(
        functools.partial(kernel, levels, heads, cores),
        out_shape=[pltpu.VMEM(flat, BF16)] * 4,
        in_specs=[in_hbm, in_hbm, in_hbm, in_vmem, in_hbm],
        out_specs=[in_vmem] * 4,
        scratch_shapes=[
            pltpu.VMEM((4,) + flat, BF16),
            pltpu.VMEM(per_head, BF16),
            pltpu.VMEM(per_head, BF16),
            pltpu.VMEM(per_head, BF16),
            pltpu.VMEM(per_head, F32),
            pltpu.VMEM(per_head, F32),
            pltpu.VMEM(per_head, F32),
            pltpu.VMEM((heads, GROUP, GROUP), BF16),
            pltpu.VMEM(per_head, F32),
            pltpu.VMEM(per_head, BF16),
            pltpu.VMEM(per_head, F32),
            pltpu.VMEM(per_head, F32),
            pltpu.VMEM((heads, DH, DH), BF16),
            pltpu.VMEM((2, heads * DH, DH), F32),
            pltpu.VMEM((2, CHUNKS, PLANE, rows, DH), F32),
            pltpu.VMEM((2, CHUNKS, PLANE, rows, DH), F32),
            pltpu.VMEM((2, CHUNKS, rows, DH), F32),
            pltpu.VMEM((2, CHUNKS, levels, rows, DH), F32),
            pltpu.VMEM((2, CHUNKS, PLANE, rows, DH), F32),
            pltpu.VMEM((2, GROUP, DH), F32),
            dma((4,)),
            dma((2, 2, CHUNKS)),
            dma((2, 2, CHUNKS)),
            dma((2, CHUNKS, levels)),
            dma((2, CHUNKS, levels)),
            dma((2,)),
        ],
        compiler_params=pltpu.CompilerParams(
            collective_id=0, has_side_effects=True, vmem_limit_bytes=60 * 1024 * 1024
        ),
    )(
        query_raw.reshape(flat),
        key_raw.reshape(flat),
        value_raw.reshape(flat),
        out_gain,
        out_grad.reshape(flat),
    )
    outs = pl.pallas_call(
        deliver,
        out_shape=[pltpu.HBM(flat, BF16)] * 4,
        in_specs=[in_vmem] * 4,
        out_specs=[in_hbm] * 4,
        scratch_shapes=[dma((4,))],
        compiler_params=pltpu.CompilerParams(vmem_limit_bytes=4 * 1024 * 1024),
    )(*outs)
    return tuple(out.reshape(tokens, heads, width) for out in outs)


def solution(mesh):
    rows = P("seq", "head", None)
    return jax.shard_map(
        body,
        mesh=mesh,
        in_specs=(rows, rows, rows, P("head", None), rows),
        out_specs=(rows,) * 4,
        check_vma=False,
    )
```

```python
import functools

import jax
import jax.numpy as jnp
from jax import lax
from jax.experimental import pallas as pl
from jax.experimental.pallas import tpu as pltpu
from jax.sharding import PartitionSpec as P

GROUP = 256
DH = 128
PLANE = 32
CHUNKS = 2
MESH = pl.DeviceIdType.MESH
F32 = jnp.float32
BF16 = jnp.bfloat16


def dot(lhs, rhs, contract):
    return lax.dot_general(lhs, rhs, (contract, ((), ())), preferred_element_type=F32)


def nn(lhs, rhs):
    return dot(lhs, rhs, ((1,), (0,)))


def nt(lhs, rhs):
    return dot(lhs, rhs, ((1,), (1,)))


def tn(lhs, rhs):
    return dot(lhs, rhs, ((0,), (0,)))


def kernel(
    levels,
    heads,
    cores,
    q_hbm,
    k_hbm,
    v_hbm,
    gain_hbm,
    g_hbm,
    normed_out,
    qg_out,
    kg_out,
    vg_out,
    raw,
    results,
    gain,
    qact,
    kact,
    vact,
    qslope,
    kslope,
    grad_in,
    attn,
    mixed,
    delta,
    dk,
    dv,
    state_b,
    own,
    gathered,
    prefix,
    total,
    z_slots,
    state,
    stats,
    in_sem,
    send_sem,
    recv_sem,
    z_send_sem,
    z_recv_sem,
    stat_sem,
    out_sem,
    ready,
):
    seq = lax.axis_index("seq")
    core = lax.axis_index("head")
    level = seq // PLANE
    place = lax.rem(seq, PLANE)
    rows = heads * DH // (CHUNKS * PLANE)
    span = heads * DH // CHUNKS
    per = heads // CHUNKS
    width = GROUP // heads

    def plane_peer(step):
        return lax.rem(place + step, PLANE)

    loads = [
        pltpu.make_async_copy(hbm, raw.at[i], in_sem.at[i])
        for i, hbm in enumerate((k_hbm, v_hbm, q_hbm, g_hbm))
    ] + [pltpu.make_async_copy(gain_hbm, gain, in_sem.at[4])]
    for load in loads:
        load.start()

    barrier = pltpu.get_barrier_semaphore()

    def greet_plane(step, carry):
        pl.semaphore_signal(
            barrier,
            inc=1,
            device_id=(level * PLANE + plane_peer(step + PLANE // 2), core),
            device_id_type=MESH,
        )
        return carry

    def greet_later(other, carry):
        pl.semaphore_signal(
            barrier, inc=1, device_id=(other * PLANE + place, core), device_id_type=MESH
        )
        return carry

    def answer_earlier(other, carry):
        pl.semaphore_signal(
            ready.at[level], inc=1, device_id=(other * PLANE + place, core), device_id_type=MESH
        )
        return carry

    lax.fori_loop(0, PLANE // 2, greet_plane, 0)
    lax.fori_loop(PLANE // 2 + 1, PLANE, greet_plane, 0)
    lax.fori_loop(level + 1, levels, greet_later, 0)
    pl.semaphore_signal(barrier, inc=1, device_id=(seq, 1 - core), device_id_type=MESH)

    row = lax.broadcasted_iota(jnp.int32, (GROUP, GROUP), 0)
    col = lax.broadcasted_iota(jnp.int32, (GROUP, GROUP), 1)
    causal = col <= row
    sort = jnp.where(col == lax.rem(row, width) * heads + row // width, 1.0, 0.0).astype(BF16)
    unsort = jnp.where(col == lax.rem(row, heads) * width + row // heads, 1.0, 0.0).astype(BF16)

    def sorted_tiles(i):
        for tile in range(heads):
            yield tile, nn(sort, raw[i, pl.ds(tile * GROUP, GROUP), :])

    def put(dst, tile, value):
        for h in range(heads):
            dst[h, pl.ds(tile * width, width), :] = value[h * width : (h + 1) * width].astype(
                dst.dtype
            )

    def activate(i, act, slope):
        for tile, value in sorted_tiles(i):
            sigma = jax.nn.sigmoid(value)
            put(act, tile, value * sigma)
            put(slope, tile, sigma * (1.0 + value * (1.0 - sigma)))

    def store(i, out, head_value):
        values = [head_value(h).astype(BF16) for h in range(heads)]
        for tile in range(heads):
            piece = jnp.concatenate(
                [value[tile * width : (tile + 1) * width] for value in values], axis=0
            )
            results[i, pl.ds(tile * GROUP, GROUP), :] = nn(unsort, piece).astype(BF16)
        copy = pltpu.make_async_copy(results.at[i], out, out_sem.at[i])
        copy.start()
        return copy

    def bytes_of(ref, sem):
        return pltpu.make_async_copy(ref, ref, sem)

    others = pl.ds(0, PLANE - 1)

    def scatter(scan, chunk):
        def send(step, carry):
            peer = plane_peer(step)
            pltpu.make_async_remote_copy(
                src_ref=own.at[scan, pl.ds(chunk * span + peer * rows, rows), :],
                dst_ref=gathered.at[scan, chunk, place],
                send_sem=send_sem.at[scan, 0, chunk],
                recv_sem=recv_sem.at[scan, 0, chunk],
                device_id=(level * PLANE + peer, core),
                device_id_type=MESH,
            ).start()
            return carry

        lax.fori_loop(1, PLANE, send, 0)
        gathered[scan, chunk, place] = own[scan, pl.ds(chunk * span + place * rows, rows), :]

    def wait_scatter(scan, chunk):
        bytes_of(gathered.at[scan, chunk, others], recv_sem.at[scan, 0, chunk]).wait()

    def wait_scatter_send(scan, chunk):
        bytes_of(gathered.at[scan, chunk, others], send_sem.at[scan, 0, chunk]).wait()

    def follows(scan, step):
        other = level + step if scan == 0 else level - step
        return (other < levels) if scan == 0 else (other >= 0), other

    def z_copy(scan, chunk, target):
        return pltpu.make_async_remote_copy(
            src_ref=total.at[scan, chunk],
            dst_ref=z_slots.at[scan, chunk, level],
            send_sem=z_send_sem.at[scan, chunk, target],
            recv_sem=z_recv_sem.at[scan, chunk, level],
            device_id=(target * PLANE + place, core),
            device_id_type=MESH,
        )

    def own_prefix(scan, chunk):
        acc = jnp.zeros((rows, DH), F32)
        order = range(PLANE) if scan == 0 else range(PLANE - 1, -1, -1)
        for p in order:
            prefix[scan, chunk, p] = acc
            acc = acc + gathered[scan, chunk, p]
        total[scan, chunk] = acc
        for step in range(1, levels):
            needed, other = follows(scan, step)

            @pl.when(needed)
            def _():
                if scan == 0 and chunk == 0:
                    pl.semaphore_wait(ready.at[other], 1)
                z_copy(scan, chunk, other).start()

    def level_prefix(scan, chunk):
        z_slots[scan, chunk, level] = jnp.zeros((rows, DH), F32)
        for source in range(levels):
            earlier = source < level if scan == 0 else source > level

            @pl.when(earlier)
            def _():
                bytes_of(
                    z_slots.at[scan, chunk, source], z_recv_sem.at[scan, chunk, source]
                ).wait()

            @pl.when(jnp.logical_not(earlier))
            def _():
                z_slots[scan, chunk, source] = jnp.zeros((rows, DH), F32)

        acc = jnp.zeros((rows, DH), F32)
        for source in range(levels):
            acc = acc + z_slots[scan, chunk, source]
        for p in range(PLANE):
            prefix[scan, chunk, p] = prefix[scan, chunk, p] + acc

    def give_back(scan, chunk):
        def send(step, carry):
            peer = plane_peer(step)
            pltpu.make_async_remote_copy(
                src_ref=prefix.at[scan, chunk, peer],
                dst_ref=state.at[scan, chunk, place],
                send_sem=send_sem.at[scan, 1, chunk],
                recv_sem=recv_sem.at[scan, 1, chunk],
                device_id=(level * PLANE + peer, core),
                device_id_type=MESH,
            ).start()
            return carry

        lax.fori_loop(1, PLANE, send, 0)
        state[scan, chunk, place] = prefix[scan, chunk, place]

    def wait_back(scan, chunk):
        bytes_of(state.at[scan, chunk, others], recv_sem.at[scan, 1, chunk]).wait()

    def drain(scan):
        for chunk in range(CHUNKS):
            wait_scatter_send(scan, chunk)
            bytes_of(state.at[scan, chunk, others], send_sem.at[scan, 1, chunk]).wait()
            for step in range(1, levels):
                needed, other = follows(scan, step)

                @pl.when(needed)
                def _():
                    z_copy(scan, chunk, other).wait_send()

    def middle(scan, work):
        for chunk in range(CHUNKS):
            wait_scatter(scan, chunk)
            own_prefix(scan, chunk)
        work()
        for chunk in range(CHUNKS):
            level_prefix(scan, chunk)
            give_back(scan, chunk)

    def scanned(scan, h):
        chunk, at = h // per, h % per
        parts = PLANE // per
        return state[scan, chunk, pl.ds(at * parts, parts)].reshape(DH, DH).astype(BF16)

    loads[0].wait()
    activate(0, kact, kslope)
    loads[1].wait()
    for tile, value in sorted_tiles(1):
        put(vact, tile, value)
    for h in range(heads):
        own[0, pl.ds(h * DH, DH), :] = tn(kact[h], vact[h])

    pl.semaphore_wait(barrier, PLANE + level)
    lax.fori_loop(0, level, answer_earlier, 0)
    for chunk in range(CHUNKS):
        scatter(0, chunk)

    loads[2].wait()
    activate(2, qact, qslope)
    for h in range(heads):
        scores = nt(qact[h], kact[h])
        attn[h] = jnp.where(causal, scores, 0.0).astype(BF16)
        mixed[h] = nn(attn[h], vact[h])

    def weigh_grad():
        loads[3].wait()
        loads[4].wait()
        for tile, value in sorted_tiles(3):
            for h in range(heads):
                grad_in[h, pl.ds(tile * width, width), :] = (
                    value[h * width : (h + 1) * width] * gain[pl.ds(h, 1), :]
                )

    middle(0, weigh_grad)

    square = jnp.zeros((GROUP, DH), F32)
    crossed = jnp.zeros((GROUP, DH), F32)
    for h in range(heads):
        if h % per == 0:
            wait_back(0, h // per)
        state_b[h] = scanned(0, h)
        value = mixed[h] + nn(qact[h], state_b[h])
        mixed[h] = value
        square = square + value * value
        crossed = crossed + grad_in[h] * value
    square = jnp.sum(square, axis=1, keepdims=True)
    crossed = jnp.sum(crossed, axis=1, keepdims=True)
    lane = lax.broadcasted_iota(jnp.int32, (GROUP, DH), 1)
    stats[0] = jnp.where(lane == 0, square, jnp.where(lane == 1, crossed, 0.0))
    exchange = pltpu.make_async_remote_copy(
        src_ref=stats.at[0],
        dst_ref=stats.at[1],
        send_sem=stat_sem.at[0],
        recv_sem=stat_sem.at[1],
        device_id=(seq, 1 - core),
        device_id_type=MESH,
    )
    exchange.start()
    exchange.wait_recv()
    both = stats[1]
    features = heads * cores * DH
    square = square + both[:, 0:1]
    crossed = crossed + both[:, 1:2]
    inv_rms = lax.rsqrt(square * (1.0 / features) + 1e-06)
    factor = crossed * (inv_rms * inv_rms * inv_rms) * (1.0 / features)
    for h in range(heads):
        delta[h] = (grad_in[h] * inv_rms - mixed[h] * factor).astype(BF16)
        own[1, pl.ds(h * DH, DH), :] = tn(qact[h], delta[h])
        if (h + 1) % per == 0:
            scatter(1, h // per)

    copies = [store(0, normed_out, lambda h: mixed[h] * inv_rms * gain[pl.ds(h, 1), :])]

    def local_grads(some_heads):
        for h in some_heads:
            bscore = jnp.where(causal, nt(delta[h], vact[h]), 0.0).astype(BF16)
            mixed[h] = (nn(bscore, kact[h]) + nt(delta[h], state_b[h])) * qslope[h]
            dk[h] = tn(bscore, qact[h])
            dv[h] = tn(attn[h], delta[h])

    local_grads(range(heads // 2))
    middle(1, lambda: None)
    local_grads(range(heads // 2, heads))
    copies.append(store(1, qg_out, lambda h: mixed[h]))
    exchange.wait_send()
    drain(0)

    for h in range(heads):
        if h % per == 0:
            wait_back(1, h // per)
        state_b[h] = scanned(1, h)
        dk[h] = (dk[h] + nt(vact[h], state_b[h])) * kslope[h]
        dv[h] = dv[h] + nn(kact[h], state_b[h])
    copies.append(store(2, kg_out, lambda h: dk[h]))
    copies.append(store(3, vg_out, lambda h: dv[h]))
    drain(1)
    for copy in copies:
        copy.wait()


def deliver(*refs):
    count = len(refs) // 2
    sems = refs[-1]
    copies = [
        pltpu.make_async_copy(refs[i], refs[count + i], sems.at[i]) for i in range(count)
    ]
    for copy in copies:
        copy.start()
    for copy in copies:
        copy.wait()


def body(query_raw, key_raw, value_raw, out_gain, out_grad):
    tokens, heads, width = query_raw.shape
    levels = lax.axis_size("seq") // PLANE
    cores = lax.axis_size("head")
    flat = (tokens * heads, width)
    rows = heads * DH // (CHUNKS * PLANE)
    anywhere = pl.BlockSpec(memory_space=pl.ANY)
    in_hbm = pl.BlockSpec(memory_space=pltpu.HBM)
    per_head = (heads, GROUP, DH)
    dma = pltpu.SemaphoreType.DMA
    outs = pl.pallas_call(
        functools.partial(kernel, levels, heads, cores),
        out_shape=[pltpu.VMEM(flat, BF16)] * 4,
        in_specs=[in_hbm] * 5,
        out_specs=[anywhere] * 4,
        scratch_shapes=[
            pltpu.VMEM((4,) + flat, BF16),
            pltpu.VMEM((4,) + flat, BF16),
            pltpu.VMEM((heads, DH), F32),
            pltpu.VMEM(per_head, BF16),
            pltpu.VMEM(per_head, BF16),
            pltpu.VMEM(per_head, BF16),
            pltpu.VMEM(per_head, F32),
            pltpu.VMEM(per_head, F32),
            pltpu.VMEM(per_head, F32),
            pltpu.VMEM((heads, GROUP, GROUP), BF16),
            pltpu.VMEM(per_head, F32),
            pltpu.VMEM(per_head, BF16),
            pltpu.VMEM(per_head, F32),
            pltpu.VMEM(per_head, F32),
            pltpu.VMEM((heads, DH, DH), BF16),
            pltpu.VMEM((2, heads * DH, DH), F32),
            pltpu.VMEM((2, CHUNKS, PLANE, rows, DH), F32),
            pltpu.VMEM((2, CHUNKS, PLANE, rows, DH), F32),
            pltpu.VMEM((2, CHUNKS, rows, DH), F32),
            pltpu.VMEM((2, CHUNKS, levels, rows, DH), F32),
            pltpu.VMEM((2, CHUNKS, PLANE, rows, DH), F32),
            pltpu.VMEM((2, GROUP, DH), F32),
            dma((5,)),
            dma((2, 2, CHUNKS)),
            dma((2, 2, CHUNKS)),
            dma((2, CHUNKS, levels)),
            dma((2, CHUNKS, levels)),
            dma((2,)),
            dma((4,)),
            pltpu.SemaphoreType.REGULAR((levels,)),
        ],
        compiler_params=pltpu.CompilerParams(
            collective_id=0, has_side_effects=True, vmem_limit_bytes=60 * 1024 * 1024
        ),
    )(
        query_raw.reshape(flat),
        key_raw.reshape(flat),
        value_raw.reshape(flat),
        out_gain,
        out_grad.reshape(flat),
    )
    outs = pl.pallas_call(
        deliver,
        out_shape=[pltpu.HBM(flat, BF16)] * 4,
        in_specs=[anywhere] * 4,
        out_specs=[in_hbm] * 4,
        scratch_shapes=[dma((4,))],
        compiler_params=pltpu.CompilerParams(vmem_limit_bytes=4 * 1024 * 1024),
    )(*outs)
    return tuple(out.reshape(tokens, heads, width) for out in outs)


def solution(mesh):
    rows = P("seq", "head", None)
    return jax.shard_map(
        body,
        mesh=mesh,
        in_specs=(rows, rows, rows, P("head", None), rows),
        out_specs=(rows,) * 4,
        check_vma=False,
    )
```

```python
import functools

import jax
import jax.numpy as jnp
from jax import lax
from jax.experimental import pallas as pl
from jax.experimental.pallas import tpu as pltpu
from jax.sharding import PartitionSpec as P

GROUP = 256
DH = 128
WIDE, LONG = 4, 8
PLANE = WIDE * LONG
CHUNKS = 2
MESH = pl.DeviceIdType.MESH
F32 = jnp.float32
BF16 = jnp.bfloat16


def dot(lhs, rhs, contract):
    return lax.dot_general(lhs, rhs, (contract, ((), ())), preferred_element_type=F32)


def nn(lhs, rhs):
    return dot(lhs, rhs, ((1,), (0,)))


def nt(lhs, rhs):
    return dot(lhs, rhs, ((1,), (1,)))


def tn(lhs, rhs):
    return dot(lhs, rhs, ((0,), (0,)))


def kernel(
    levels,
    heads,
    cores,
    q_hbm,
    k_hbm,
    v_hbm,
    gain_hbm,
    g_hbm,
    normed_out,
    qg_out,
    kg_out,
    vg_out,
    raw,
    results,
    gain,
    qact,
    qact_t,
    kact,
    vact,
    qslope,
    kslope,
    grad_in,
    attn,
    mixed,
    delta,
    dk,
    dv,
    state_b,
    own,
    gathered,
    prefix,
    total,
    z_slots,
    state,
    stats,
    in_sem,
    send_sem,
    recv_sem,
    z_send_sem,
    z_recv_sem,
    stat_sem,
    out_sem,
    ready,
):
    seq = lax.axis_index("seq")
    core = lax.axis_index("head")
    level = seq // PLANE
    place = lax.rem(seq, PLANE)
    rows = heads * DH // (CHUNKS * PLANE)
    span = heads * DH // CHUNKS
    per = heads // CHUNKS
    width = GROUP // heads

    across, along = place // LONG, lax.rem(place, LONG)

    def each_peer(act):
        half = LONG // 2
        steps = [half]
        for off in range(1, half):
            steps += [half - off, half + off]

        for step in steps + [0]:

            def one(turn, carry, step=step):
                x = lax.rem(across + lax.rem(turn + WIDE // 2, WIDE), WIDE)
                act(x * LONG + lax.rem(along + step, LONG))
                return carry

            if step:
                lax.fori_loop(0, WIDE, one, 0)
            else:
                lax.fori_loop(0, WIDE // 2, one, 0)
                lax.fori_loop(WIDE // 2 + 1, WIDE, one, 0)

    loads = [
        pltpu.make_async_copy(hbm, raw.at[i], in_sem.at[i])
        for i, hbm in enumerate((k_hbm, v_hbm, q_hbm, g_hbm))
    ] + [pltpu.make_async_copy(gain_hbm, gain, in_sem.at[4])]
    for load in loads:
        load.start()

    barrier = pltpu.get_barrier_semaphore()

    def greet(peer):
        pl.semaphore_signal(
            barrier, inc=1, device_id=(level * PLANE + peer, core), device_id_type=MESH
        )

    def greet_later(other, carry):
        pl.semaphore_signal(
            barrier, inc=1, device_id=(other * PLANE + place, core), device_id_type=MESH
        )
        return carry

    def answer_earlier(other, carry):
        pl.semaphore_signal(
            ready.at[level], inc=1, device_id=(other * PLANE + place, core), device_id_type=MESH
        )
        return carry

    each_peer(greet)
    lax.fori_loop(level + 1, levels, greet_later, 0)
    pl.semaphore_signal(barrier, inc=1, device_id=(seq, 1 - core), device_id_type=MESH)

    row = lax.broadcasted_iota(jnp.int32, (GROUP, GROUP), 0)
    col = lax.broadcasted_iota(jnp.int32, (GROUP, GROUP), 1)
    causal = col <= row
    sort = jnp.where(col == lax.rem(row, width) * heads + row // width, 1.0, 0.0).astype(BF16)
    unsort = jnp.where(col == lax.rem(row, heads) * width + row // heads, 1.0, 0.0).astype(BF16)

    def sorted_tiles(i):
        for tile in range(heads):
            yield tile, nn(sort, raw[i, pl.ds(tile * GROUP, GROUP), :])

    def put(dst, tile, value):
        for h in range(heads):
            dst[h, pl.ds(tile * width, width), :] = value[h * width : (h + 1) * width].astype(
                dst.dtype
            )

    def activate(i, act, slope):
        for tile, value in sorted_tiles(i):
            sigma = jax.nn.sigmoid(value)
            put(act, tile, value * sigma)
            put(slope, tile, sigma * (1.0 + value * (1.0 - sigma)))

    def store(i, out, head_value):
        values = [head_value(h).astype(BF16) for h in range(heads)]
        for tile in range(heads):
            piece = jnp.concatenate(
                [value[tile * width : (tile + 1) * width] for value in values], axis=0
            )
            results[i, pl.ds(tile * GROUP, GROUP), :] = nn(unsort, piece).astype(BF16)
        copy = pltpu.make_async_copy(results.at[i], out, out_sem.at[i])
        copy.start()
        return copy

    def bytes_of(ref, sem):
        return pltpu.make_async_copy(ref, ref, sem)

    others = pl.ds(0, PLANE - 1)

    def scatter(scan, chunk):
        def send(peer):
            pltpu.make_async_remote_copy(
                src_ref=own.at[scan, pl.ds(chunk * span + peer * rows, rows), :],
                dst_ref=gathered.at[scan, chunk, place],
                send_sem=send_sem.at[scan, 0, chunk],
                recv_sem=recv_sem.at[scan, 0, chunk],
                device_id=(level * PLANE + peer, core),
                device_id_type=MESH,
            ).start()

        each_peer(send)
        gathered[scan, chunk, place] = own[scan, pl.ds(chunk * span + place * rows, rows), :]

    def wait_scatter(scan, chunk):
        bytes_of(gathered.at[scan, chunk, others], recv_sem.at[scan, 0, chunk]).wait()

    def wait_scatter_send(scan, chunk):
        bytes_of(gathered.at[scan, chunk, others], send_sem.at[scan, 0, chunk]).wait()

    needing = ((level + 1, levels), (0, level))
    needed = ((0, level), (level + 1, levels))

    def z_copy(scan, chunk, target):
        return pltpu.make_async_remote_copy(
            src_ref=total.at[scan, chunk],
            dst_ref=z_slots.at[scan, chunk, level],
            send_sem=z_send_sem.at[scan, chunk, target],
            recv_sem=z_recv_sem.at[scan, chunk, level],
            device_id=(target * PLANE + place, core),
            device_id_type=MESH,
        )

    def own_total(scan, chunk):
        acc = gathered[scan, chunk, 0]
        for p in range(1, PLANE):
            acc = acc + gathered[scan, chunk, p]
        total[scan, chunk] = acc

        def send(target, carry):
            if scan == 0 and chunk == 0:
                pl.semaphore_wait(ready.at[target], 1)
            z_copy(scan, chunk, target).start()
            return carry

        lax.fori_loop(*needing[scan], send, 0)

    def all_prefixes(scan, chunk):
        def take(source, acc):
            bytes_of(z_slots.at[scan, chunk, source], z_recv_sem.at[scan, chunk, source]).wait()
            return acc + z_slots[scan, chunk, source]

        acc = lax.fori_loop(*needed[scan], take, jnp.zeros((rows, DH), F32))
        for p in range(PLANE) if scan == 0 else range(PLANE - 1, -1, -1):
            prefix[scan, chunk, p] = acc
            acc = acc + gathered[scan, chunk, p]

    def give_back(scan, chunk):
        def send(peer):
            pltpu.make_async_remote_copy(
                src_ref=prefix.at[scan, chunk, peer],
                dst_ref=state.at[scan, chunk, place],
                send_sem=send_sem.at[scan, 1, chunk],
                recv_sem=recv_sem.at[scan, 1, chunk],
                device_id=(level * PLANE + peer, core),
                device_id_type=MESH,
            ).start()

        each_peer(send)
        state[scan, chunk, place] = prefix[scan, chunk, place]

    def wait_back(scan, chunk):
        bytes_of(state.at[scan, chunk, others], recv_sem.at[scan, 1, chunk]).wait()

    def drain(scan):
        for chunk in range(CHUNKS):
            wait_scatter_send(scan, chunk)
            bytes_of(state.at[scan, chunk, others], send_sem.at[scan, 1, chunk]).wait()

            def sent(target, carry):
                z_copy(scan, chunk, target).wait_send()
                return carry

            lax.fori_loop(*needing[scan], sent, 0)

    def middle(scan, work):
        for chunk in range(CHUNKS):
            wait_scatter(scan, chunk)
            own_total(scan, chunk)
        work()
        for chunk in range(CHUNKS):
            all_prefixes(scan, chunk)
            give_back(scan, chunk)

    def scanned(scan, h):
        chunk, at = h // per, h % per
        parts = PLANE // per
        return state[scan, chunk, pl.ds(at * parts, parts)].reshape(DH, DH).astype(BF16)

    loads[0].wait()
    activate(0, kact, kslope)
    loads[1].wait()
    for tile, value in sorted_tiles(1):
        put(vact, tile, value)
    for h in range(heads):
        own[0, pl.ds(h * DH, DH), :] = tn(kact[h], vact[h])

    pl.semaphore_wait(barrier, PLANE + level)
    lax.fori_loop(0, level, answer_earlier, 0)
    for chunk in range(CHUNKS):
        scatter(0, chunk)

    loads[2].wait()
    activate(2, qact, qslope)
    for h in range(heads):
        qact_t[h] = qact[h].T
        scores = nt(qact[h], kact[h])
        attn[h] = jnp.where(causal, scores, 0.0).astype(BF16)
        mixed[h] = nn(attn[h], vact[h])

    def weigh_grad():
        loads[3].wait()
        loads[4].wait()
        for tile, value in sorted_tiles(3):
            for h in range(heads):
                grad_in[h, pl.ds(tile * width, width), :] = (
                    value[h * width : (h + 1) * width] * gain[pl.ds(h, 1), :]
                )

    middle(0, weigh_grad)

    square = jnp.zeros((GROUP, DH), F32)
    crossed = jnp.zeros((GROUP, DH), F32)
    for h in range(heads):
        if h % per == 0:
            wait_back(0, h // per)
        state_b[h] = scanned(0, h)
        value = mixed[h] + nn(qact[h], state_b[h])
        mixed[h] = value
        square = square + value * value
        crossed = crossed + grad_in[h] * value
    square = jnp.sum(square, axis=1, keepdims=True)
    crossed = jnp.sum(crossed, axis=1, keepdims=True)
    lane = lax.broadcasted_iota(jnp.int32, (GROUP, DH), 1)
    stats[0] = jnp.where(lane == 0, square, jnp.where(lane == 1, crossed, 0.0))
    exchange = pltpu.make_async_remote_copy(
        src_ref=stats.at[0],
        dst_ref=stats.at[1],
        send_sem=stat_sem.at[0],
        recv_sem=stat_sem.at[1],
        device_id=(seq, 1 - core),
        device_id_type=MESH,
    )
    exchange.start()
    exchange.wait_recv()
    both = stats[1]
    features = heads * cores * DH
    square = square + both[:, 0:1]
    crossed = crossed + both[:, 1:2]
    inv_rms = lax.rsqrt(square * (1.0 / features) + 1e-06)
    factor = crossed * (inv_rms * inv_rms * inv_rms) * (1.0 / features)
    for h in range(heads):
        delta[h] = (grad_in[h] * inv_rms - mixed[h] * factor).astype(BF16)
        own[1, pl.ds(h * DH, DH), :] = nn(qact_t[h], delta[h])
        if (h + 1) % per == 0:
            scatter(1, h // per)

    copies = [store(0, normed_out, lambda h: mixed[h] * inv_rms * gain[pl.ds(h, 1), :])]

    def local_grads(some_heads):
        for h in some_heads:
            bscore = jnp.where(causal, nt(delta[h], vact[h]), 0.0).astype(BF16)
            mixed[h] = (nn(bscore, kact[h]) + nt(delta[h], state_b[h])) * qslope[h]
            dk[h] = tn(bscore, qact[h])
            dv[h] = tn(attn[h], delta[h])

    local_grads(range(heads // 2))
    middle(1, lambda: None)
    local_grads(range(heads // 2, heads))
    copies.append(store(1, qg_out, lambda h: mixed[h]))
    exchange.wait_send()
    drain(0)

    for h in range(heads):
        if h % per == 0:
            wait_back(1, h // per)
        state_b[h] = scanned(1, h)
        dk[h] = (dk[h] + nt(vact[h], state_b[h])) * kslope[h]
        dv[h] = dv[h] + nn(kact[h], state_b[h])
    copies.append(store(2, kg_out, lambda h: dk[h]))
    copies.append(store(3, vg_out, lambda h: dv[h]))
    drain(1)
    for copy in copies:
        copy.wait()


def deliver(*refs):
    count = len(refs) // 2
    sems = refs[-1]
    copies = [
        pltpu.make_async_copy(refs[i], refs[count + i], sems.at[i]) for i in range(count)
    ]
    for copy in copies:
        copy.start()
    for copy in copies:
        copy.wait()


def body(query_raw, key_raw, value_raw, out_gain, out_grad):
    tokens, heads, width = query_raw.shape
    levels = lax.axis_size("seq") // PLANE
    cores = lax.axis_size("head")
    flat = (tokens * heads, width)
    rows = heads * DH // (CHUNKS * PLANE)
    anywhere = pl.BlockSpec(memory_space=pl.ANY)
    in_hbm = pl.BlockSpec(memory_space=pltpu.HBM)
    per_head = (heads, GROUP, DH)
    dma = pltpu.SemaphoreType.DMA
    outs = pl.pallas_call(
        functools.partial(kernel, levels, heads, cores),
        out_shape=[pltpu.VMEM(flat, BF16)] * 4,
        in_specs=[in_hbm] * 5,
        out_specs=[anywhere] * 4,
        scratch_shapes=[
            pltpu.VMEM((4,) + flat, BF16),
            pltpu.VMEM((4,) + flat, BF16),
            pltpu.VMEM((heads, DH), F32),
            pltpu.VMEM(per_head, BF16),
            pltpu.VMEM((heads, DH, GROUP), BF16),
            pltpu.VMEM(per_head, BF16),
            pltpu.VMEM(per_head, BF16),
            pltpu.VMEM(per_head, F32),
            pltpu.VMEM(per_head, F32),
            pltpu.VMEM(per_head, F32),
            pltpu.VMEM((heads, GROUP, GROUP), BF16),
            pltpu.VMEM(per_head, F32),
            pltpu.VMEM(per_head, BF16),
            pltpu.VMEM(per_head, F32),
            pltpu.VMEM(per_head, F32),
            pltpu.VMEM((heads, DH, DH), BF16),
            pltpu.VMEM((2, heads * DH, DH), F32),
            pltpu.VMEM((2, CHUNKS, PLANE, rows, DH), F32),
            pltpu.VMEM((2, CHUNKS, PLANE, rows, DH), F32),
            pltpu.VMEM((2, CHUNKS, rows, DH), F32),
            pltpu.VMEM((2, CHUNKS, levels, rows, DH), F32),
            pltpu.VMEM((2, CHUNKS, PLANE, rows, DH), F32),
            pltpu.VMEM((2, GROUP, DH), F32),
            dma((5,)),
            dma((2, 2, CHUNKS)),
            dma((2, 2, CHUNKS)),
            dma((2, CHUNKS, levels)),
            dma((2, CHUNKS, levels)),
            dma((2,)),
            dma((4,)),
            pltpu.SemaphoreType.REGULAR((levels,)),
        ],
        compiler_params=pltpu.CompilerParams(
            collective_id=0, has_side_effects=True, vmem_limit_bytes=60 * 1024 * 1024
        ),
    )(
        query_raw.reshape(flat),
        key_raw.reshape(flat),
        value_raw.reshape(flat),
        out_gain,
        out_grad.reshape(flat),
    )
    outs = pl.pallas_call(
        deliver,
        out_shape=[pltpu.HBM(flat, BF16)] * 4,
        in_specs=[anywhere] * 4,
        out_specs=[in_hbm] * 4,
        scratch_shapes=[dma((4,))],
        compiler_params=pltpu.CompilerParams(vmem_limit_bytes=4 * 1024 * 1024),
    )(*outs)
    return tuple(out.reshape(tokens, heads, width) for out in outs)


def solution(mesh):
    rows = P("seq", "head", None)
    return jax.shard_map(
        body,
        mesh=mesh,
        in_specs=(rows, rows, rows, P("head", None), rows),
        out_specs=(rows,) * 4,
        check_vma=False,
    )
```

```python
import functools

import jax
import jax.numpy as jnp
from jax import lax
from jax.experimental import pallas as pl
from jax.experimental.pallas import tpu as pltpu
from jax.sharding import PartitionSpec as P

GROUP = 256
DH = 128
WIDE, LONG = 4, 8
PLANE = WIDE * LONG
CHUNKS = 2
MESH = pl.DeviceIdType.MESH
F32 = jnp.float32
BF16 = jnp.bfloat16


def dot(lhs, rhs, contract):
    return lax.dot_general(lhs, rhs, (contract, ((), ())), preferred_element_type=F32)


def nn(lhs, rhs):
    return dot(lhs, rhs, ((1,), (0,)))


def nt(lhs, rhs):
    return dot(lhs, rhs, ((1,), (1,)))


def tn(lhs, rhs):
    return dot(lhs, rhs, ((0,), (0,)))


def kernel(
    levels,
    heads,
    cores,
    q_hbm,
    k_hbm,
    v_hbm,
    gain_hbm,
    g_hbm,
    normed_out,
    qg_out,
    kg_out,
    vg_out,
    raw,
    results,
    gain,
    qact,
    qact_t,
    kact,
    vact,
    qslope,
    kslope,
    grad_in,
    attn,
    mixed,
    delta,
    dk,
    dv,
    state_b,
    own,
    gathered,
    prefix,
    total,
    z_slots,
    state,
    stats,
    in_sem,
    send_sem,
    recv_sem,
    z_send_sem,
    z_recv_sem,
    stat_sem,
    out_sem,
    ready,
    ready_plane,
    ready_core,
):
    seq = lax.axis_index("seq")
    core = lax.axis_index("head")
    level = seq // PLANE
    place = lax.rem(seq, PLANE)
    rows = heads * DH // (CHUNKS * PLANE)
    span = heads * DH // CHUNKS
    per = heads // CHUNKS
    width = GROUP // heads

    across, along = place // LONG, lax.rem(place, LONG)

    def rank_of(peer):
        x, y = peer // LONG, lax.rem(peer, LONG)
        back = y // (LONG // 2)
        return (y + back * (LONG + LONG // 2 - 1 - 2 * y)) * WIDE + x

    rank = rank_of(place)

    def each_peer(act):
        half = LONG // 2
        steps = [half]
        for off in range(1, half):
            steps += [half - off, half + off]

        for step in steps + [0]:

            def one(turn, carry, step=step):
                x = lax.rem(across + lax.rem(turn + WIDE // 2, WIDE), WIDE)
                act(x * LONG + lax.rem(along + step, LONG))
                return carry

            if step:
                lax.fori_loop(0, WIDE, one, 0)
            else:
                lax.fori_loop(0, WIDE // 2, one, 0)
                lax.fori_loop(WIDE // 2 + 1, WIDE, one, 0)

    loads = [
        pltpu.make_async_copy(hbm, raw.at[i], in_sem.at[i])
        for i, hbm in enumerate((k_hbm, v_hbm, q_hbm, g_hbm))
    ] + [pltpu.make_async_copy(gain_hbm, gain, in_sem.at[4])]
    for load in loads:
        load.start()

    barrier = pltpu.get_barrier_semaphore()

    def greet(peer):
        @pl.when(rank_of(peer) > rank)
        def _():
            pl.semaphore_signal(
                barrier, inc=1, device_id=(level * PLANE + peer, core), device_id_type=MESH
            )

    def greet_later(other, carry):
        pl.semaphore_signal(
            barrier, inc=1, device_id=(other * PLANE + place, core), device_id_type=MESH
        )
        return carry

    def answer(peer):
        @pl.when(rank_of(peer) < rank)
        def _():
            pl.semaphore_signal(
                ready_plane.at[place],
                inc=1,
                device_id=(level * PLANE + peer, core),
                device_id_type=MESH,
            )

    def answer_earlier(other, carry):
        pl.semaphore_signal(
            ready.at[level], inc=1, device_id=(other * PLANE + place, core), device_id_type=MESH
        )
        return carry

    each_peer(greet)
    lax.fori_loop(level + 1, levels, greet_later, 0)

    @pl.when(core == 0)
    def _():
        pl.semaphore_signal(barrier, inc=1, device_id=(seq, 1 - core), device_id_type=MESH)

    row = lax.broadcasted_iota(jnp.int32, (GROUP, GROUP), 0)
    col = lax.broadcasted_iota(jnp.int32, (GROUP, GROUP), 1)
    causal = col <= row
    sort = jnp.where(col == lax.rem(row, width) * heads + row // width, 1.0, 0.0).astype(BF16)
    unsort = jnp.where(col == lax.rem(row, heads) * width + row // heads, 1.0, 0.0).astype(BF16)

    def sorted_tiles(i):
        for tile in range(heads):
            yield tile, nn(sort, raw[i, pl.ds(tile * GROUP, GROUP), :])

    def put(dst, tile, value):
        for h in range(heads):
            dst[h, pl.ds(tile * width, width), :] = value[h * width : (h + 1) * width].astype(
                dst.dtype
            )

    def activate(i, act, slope):
        for tile, value in sorted_tiles(i):
            sigma = jax.nn.sigmoid(value)
            put(act, tile, value * sigma)
            put(slope, tile, sigma * (1.0 + value * (1.0 - sigma)))

    def store(i, out, head_value):
        values = [head_value(h).astype(BF16) for h in range(heads)]
        for tile in range(heads):
            piece = jnp.concatenate(
                [value[tile * width : (tile + 1) * width] for value in values], axis=0
            )
            results[i, pl.ds(tile * GROUP, GROUP), :] = nn(unsort, piece).astype(BF16)
        copy = pltpu.make_async_copy(results.at[i], out, out_sem.at[i])
        copy.start()
        return copy

    def bytes_of(ref, sem):
        return pltpu.make_async_copy(ref, ref, sem)

    others = pl.ds(0, PLANE - 1)

    def send_slice(scan, chunk, peer):
        pltpu.make_async_remote_copy(
            src_ref=own.at[scan, pl.ds(chunk * span + peer * rows, rows), :],
            dst_ref=gathered.at[scan, chunk, place],
            send_sem=send_sem.at[scan, 0, chunk],
            recv_sem=recv_sem.at[scan, 0, chunk],
            device_id=(level * PLANE + peer, core),
            device_id_type=MESH,
        ).start()

    def keep_slice(scan, chunk):
        gathered[scan, chunk, place] = own[scan, pl.ds(chunk * span + place * rows, rows), :]

    def scatter(scan, chunk):
        each_peer(lambda peer: send_slice(scan, chunk, peer))
        keep_slice(scan, chunk)

    def first_scatter():
        for chunk in range(CHUNKS):

            def to_earlier(peer):
                @pl.when(rank_of(peer) < rank)
                def _():
                    send_slice(0, chunk, peer)

            each_peer(to_earlier)

        def to_later(peer):
            @pl.when(rank_of(peer) > rank)
            def _():
                pl.semaphore_wait(ready_plane.at[peer], 1)
                for chunk in range(CHUNKS):
                    send_slice(0, chunk, peer)

        each_peer(to_later)
        for chunk in range(CHUNKS):
            keep_slice(0, chunk)

    def wait_scatter(scan, chunk):
        bytes_of(gathered.at[scan, chunk, others], recv_sem.at[scan, 0, chunk]).wait()

    def wait_scatter_send(scan, chunk):
        bytes_of(gathered.at[scan, chunk, others], send_sem.at[scan, 0, chunk]).wait()

    needing = ((level + 1, levels), (0, level))
    needed = ((0, level), (level + 1, levels))

    def z_copy(scan, chunk, target):
        return pltpu.make_async_remote_copy(
            src_ref=total.at[scan, chunk],
            dst_ref=z_slots.at[scan, chunk, level],
            send_sem=z_send_sem.at[scan, chunk, target],
            recv_sem=z_recv_sem.at[scan, chunk, level],
            device_id=(target * PLANE + place, core),
            device_id_type=MESH,
        )

    def own_total(scan, chunk):
        acc = gathered[scan, chunk, 0]
        for p in range(1, PLANE):
            acc = acc + gathered[scan, chunk, p]
        total[scan, chunk] = acc

        def send(target, carry):
            if scan == 0 and chunk == 0:
                pl.semaphore_wait(ready.at[target], 1)
            z_copy(scan, chunk, target).start()
            return carry

        lax.fori_loop(*needing[scan], send, 0)

    def all_prefixes(scan, chunk):
        def take(source, acc):
            bytes_of(z_slots.at[scan, chunk, source], z_recv_sem.at[scan, chunk, source]).wait()
            return acc + z_slots[scan, chunk, source]

        acc = lax.fori_loop(*needed[scan], take, jnp.zeros((rows, DH), F32))
        for p in range(PLANE) if scan == 0 else range(PLANE - 1, -1, -1):
            prefix[scan, chunk, p] = acc
            acc = acc + gathered[scan, chunk, p]

    def give_back(scan, chunk):
        def send(peer):
            pltpu.make_async_remote_copy(
                src_ref=prefix.at[scan, chunk, peer],
                dst_ref=state.at[scan, chunk, place],
                send_sem=send_sem.at[scan, 1, chunk],
                recv_sem=recv_sem.at[scan, 1, chunk],
                device_id=(level * PLANE + peer, core),
                device_id_type=MESH,
            ).start()

        each_peer(send)
        state[scan, chunk, place] = prefix[scan, chunk, place]

    def wait_back(scan, chunk):
        bytes_of(state.at[scan, chunk, others], recv_sem.at[scan, 1, chunk]).wait()

    def drain(scan):
        for chunk in range(CHUNKS):
            wait_scatter_send(scan, chunk)
            bytes_of(state.at[scan, chunk, others], send_sem.at[scan, 1, chunk]).wait()

            def sent(target, carry):
                z_copy(scan, chunk, target).wait_send()
                return carry

            lax.fori_loop(*needing[scan], sent, 0)

    def middle(scan, work):
        for chunk in range(CHUNKS):
            wait_scatter(scan, chunk)
            own_total(scan, chunk)
        work()
        for chunk in range(CHUNKS):
            all_prefixes(scan, chunk)
            give_back(scan, chunk)

    def scanned(scan, h):
        chunk, at = h // per, h % per
        parts = PLANE // per
        return state[scan, chunk, pl.ds(at * parts, parts)].reshape(DH, DH).astype(BF16)

    loads[0].wait()
    activate(0, kact, kslope)
    loads[1].wait()
    for tile, value in sorted_tiles(1):
        put(vact, tile, value)
    for h in range(heads):
        own[0, pl.ds(h * DH, DH), :] = tn(kact[h], vact[h])

    earlier = rank + level + core

    @pl.when(earlier > 0)
    def _():
        pl.semaphore_wait(barrier, earlier)

    lax.fori_loop(0, level, answer_earlier, 0)
    each_peer(answer)

    @pl.when(core == 1)
    def _():
        pl.semaphore_signal(ready_core, inc=1, device_id=(seq, 1 - core), device_id_type=MESH)

    first_scatter()

    loads[2].wait()
    activate(2, qact, qslope)
    for h in range(heads):
        qact_t[h] = qact[h].T
        scores = nt(qact[h], kact[h])
        attn[h] = jnp.where(causal, scores, 0.0).astype(BF16)
        mixed[h] = nn(attn[h], vact[h])

    def weigh_grad():
        loads[3].wait()
        loads[4].wait()
        for tile, value in sorted_tiles(3):
            for h in range(heads):
                grad_in[h, pl.ds(tile * width, width), :] = (
                    value[h * width : (h + 1) * width] * gain[pl.ds(h, 1), :]
                )

    middle(0, weigh_grad)

    square = jnp.zeros((GROUP, DH), F32)
    crossed = jnp.zeros((GROUP, DH), F32)
    for h in range(heads):
        if h % per == 0:
            wait_back(0, h // per)
        state_b[h] = scanned(0, h)
        value = mixed[h] + nn(qact[h], state_b[h])
        mixed[h] = value
        square = square + value * value
        crossed = crossed + grad_in[h] * value
    square = jnp.sum(square, axis=1, keepdims=True)
    crossed = jnp.sum(crossed, axis=1, keepdims=True)
    lane = lax.broadcasted_iota(jnp.int32, (GROUP, DH), 1)
    stats[0] = jnp.where(lane == 0, square, jnp.where(lane == 1, crossed, 0.0))
    exchange = pltpu.make_async_remote_copy(
        src_ref=stats.at[0],
        dst_ref=stats.at[1],
        send_sem=stat_sem.at[0],
        recv_sem=stat_sem.at[1],
        device_id=(seq, 1 - core),
        device_id_type=MESH,
    )

    @pl.when(core == 0)
    def _():
        pl.semaphore_wait(ready_core, 1)

    exchange.start()
    exchange.wait_recv()
    both = stats[1]
    features = heads * cores * DH
    square = square + both[:, 0:1]
    crossed = crossed + both[:, 1:2]
    inv_rms = lax.rsqrt(square * (1.0 / features) + 1e-06)
    factor = crossed * (inv_rms * inv_rms * inv_rms) * (1.0 / features)
    for h in range(heads):
        delta[h] = (grad_in[h] * inv_rms - mixed[h] * factor).astype(BF16)
        own[1, pl.ds(h * DH, DH), :] = nn(qact_t[h], delta[h])
        if (h + 1) % per == 0:
            scatter(1, h // per)

    copies = [store(0, normed_out, lambda h: mixed[h] * inv_rms * gain[pl.ds(h, 1), :])]

    def local_grads(some_heads):
        for h in some_heads:
            bscore = jnp.where(causal, nt(delta[h], vact[h]), 0.0).astype(BF16)
            mixed[h] = (nn(bscore, kact[h]) + nt(delta[h], state_b[h])) * qslope[h]
            dk[h] = tn(bscore, qact[h])
            dv[h] = tn(attn[h], delta[h])

    local_grads(range(heads // 2))
    middle(1, lambda: None)
    local_grads(range(heads // 2, heads))
    copies.append(store(1, qg_out, lambda h: mixed[h]))
    exchange.wait_send()
    drain(0)

    for h in range(heads):
        if h % per == 0:
            wait_back(1, h // per)
        state_b[h] = scanned(1, h)
        dk[h] = (dk[h] + nt(vact[h], state_b[h])) * kslope[h]
        dv[h] = dv[h] + nn(kact[h], state_b[h])
    copies.append(store(2, kg_out, lambda h: dk[h]))
    copies.append(store(3, vg_out, lambda h: dv[h]))
    drain(1)
    for copy in copies:
        copy.wait()


def deliver(*refs):
    count = len(refs) // 2
    sems = refs[-1]
    copies = [
        pltpu.make_async_copy(refs[i], refs[count + i], sems.at[i]) for i in range(count)
    ]
    for copy in copies:
        copy.start()
    for copy in copies:
        copy.wait()


def body(query_raw, key_raw, value_raw, out_gain, out_grad):
    tokens, heads, width = query_raw.shape
    levels = lax.axis_size("seq") // PLANE
    cores = lax.axis_size("head")
    flat = (tokens * heads, width)
    rows = heads * DH // (CHUNKS * PLANE)
    anywhere = pl.BlockSpec(memory_space=pl.ANY)
    in_hbm = pl.BlockSpec(memory_space=pltpu.HBM)
    per_head = (heads, GROUP, DH)
    dma = pltpu.SemaphoreType.DMA
    outs = pl.pallas_call(
        functools.partial(kernel, levels, heads, cores),
        out_shape=[pltpu.VMEM(flat, BF16)] * 4,
        in_specs=[in_hbm] * 5,
        out_specs=[anywhere] * 4,
        scratch_shapes=[
            pltpu.VMEM((4,) + flat, BF16),
            pltpu.VMEM((4,) + flat, BF16),
            pltpu.VMEM((heads, DH), F32),
            pltpu.VMEM(per_head, BF16),
            pltpu.VMEM((heads, DH, GROUP), BF16),
            pltpu.VMEM(per_head, BF16),
            pltpu.VMEM(per_head, BF16),
            pltpu.VMEM(per_head, F32),
            pltpu.VMEM(per_head, F32),
            pltpu.VMEM(per_head, F32),
            pltpu.VMEM((heads, GROUP, GROUP), BF16),
            pltpu.VMEM(per_head, F32),
            pltpu.VMEM(per_head, BF16),
            pltpu.VMEM(per_head, F32),
            pltpu.VMEM(per_head, F32),
            pltpu.VMEM((heads, DH, DH), BF16),
            pltpu.VMEM((2, heads * DH, DH), F32),
            pltpu.VMEM((2, CHUNKS, PLANE, rows, DH), F32),
            pltpu.VMEM((2, CHUNKS, PLANE, rows, DH), F32),
            pltpu.VMEM((2, CHUNKS, rows, DH), F32),
            pltpu.VMEM((2, CHUNKS, levels, rows, DH), F32),
            pltpu.VMEM((2, CHUNKS, PLANE, rows, DH), F32),
            pltpu.VMEM((2, GROUP, DH), F32),
            dma((5,)),
            dma((2, 2, CHUNKS)),
            dma((2, 2, CHUNKS)),
            dma((2, CHUNKS, levels)),
            dma((2, CHUNKS, levels)),
            dma((2,)),
            dma((4,)),
            pltpu.SemaphoreType.REGULAR((levels,)),
            pltpu.SemaphoreType.REGULAR((PLANE,)),
            pltpu.SemaphoreType.REGULAR,
        ],
        compiler_params=pltpu.CompilerParams(
            collective_id=0, has_side_effects=True, vmem_limit_bytes=60 * 1024 * 1024
        ),
    )(
        query_raw.reshape(flat),
        key_raw.reshape(flat),
        value_raw.reshape(flat),
        out_gain,
        out_grad.reshape(flat),
    )
    outs = pl.pallas_call(
        deliver,
        out_shape=[pltpu.HBM(flat, BF16)] * 4,
        in_specs=[anywhere] * 4,
        out_specs=[in_hbm] * 4,
        scratch_shapes=[dma((4,))],
        compiler_params=pltpu.CompilerParams(vmem_limit_bytes=4 * 1024 * 1024),
    )(*outs)
    return tuple(out.reshape(tokens, heads, width) for out in outs)


def solution(mesh):
    rows = P("seq", "head", None)
    return jax.shard_map(
        body,
        mesh=mesh,
        in_specs=(rows, rows, rows, P("head", None), rows),
        out_specs=(rows,) * 4,
        check_vma=False,
    )
```

```python
import functools

import jax
import jax.numpy as jnp
from jax import lax
from jax.experimental import pallas as pl
from jax.experimental.pallas import tpu as pltpu
from jax.sharding import PartitionSpec as P

GROUP = 256
DH = 128
WIDE, LONG = 4, 8
PLANE = WIDE * LONG
CHUNKS = 2
MESH = pl.DeviceIdType.MESH
F32 = jnp.float32
BF16 = jnp.bfloat16


def dot(lhs, rhs, contract):
    return lax.dot_general(lhs, rhs, (contract, ((), ())), preferred_element_type=F32)


def nn(lhs, rhs):
    return dot(lhs, rhs, ((1,), (0,)))


def nt(lhs, rhs):
    return dot(lhs, rhs, ((1,), (1,)))


def tn(lhs, rhs):
    return dot(lhs, rhs, ((0,), (0,)))


def kernel(
    levels,
    heads,
    cores,
    q_hbm,
    k_hbm,
    v_hbm,
    gain_hbm,
    g_hbm,
    normed_out,
    qg_out,
    kg_out,
    vg_out,
    raw,
    results,
    gain,
    qact,
    qact_t,
    kact,
    vact,
    qslope,
    kslope,
    grad_in,
    attn,
    mixed,
    delta,
    dk,
    dv,
    state_b,
    own,
    gathered,
    prefix,
    total,
    z_slots,
    state,
    stats,
    in_sem,
    send_sem,
    recv_sem,
    z_send_sem,
    z_recv_sem,
    stat_sem,
    out_sem,
    ready,
):
    seq = lax.axis_index("seq")
    core = lax.axis_index("head")
    level = seq // PLANE
    place = lax.rem(seq, PLANE)
    rows = heads * DH // (CHUNKS * PLANE)
    span = heads * DH // CHUNKS
    per = heads // CHUNKS
    width = GROUP // heads

    across, along = place // LONG, lax.rem(place, LONG)

    def each_peer(act):
        half = LONG // 2
        steps = [half]
        for off in range(1, half):
            steps += [half - off, half + off]

        for step in steps + [0]:

            def one(turn, carry, step=step):
                x = lax.rem(across + lax.rem(turn + WIDE // 2, WIDE), WIDE)
                act(x * LONG + lax.rem(along + step, LONG))
                return carry

            if step:
                lax.fori_loop(0, WIDE, one, 0)
            else:
                lax.fori_loop(0, WIDE // 2, one, 0)
                lax.fori_loop(WIDE // 2 + 1, WIDE, one, 0)

    barrier = pltpu.get_barrier_semaphore()

    def greet(peer):
        pl.semaphore_signal(
            barrier, inc=1, device_id=(level * PLANE + peer, core), device_id_type=MESH
        )

    def greet_later(other, carry):
        pl.semaphore_signal(
            barrier, inc=1, device_id=(other * PLANE + place, core), device_id_type=MESH
        )
        return carry

    def answer_earlier(other, carry):
        pl.semaphore_signal(
            ready.at[level], inc=1, device_id=(other * PLANE + place, core), device_id_type=MESH
        )
        return carry

    each_peer(greet)
    loads = [
        pltpu.make_async_copy(hbm, raw.at[i], in_sem.at[i])
        for i, hbm in enumerate((k_hbm, v_hbm, q_hbm, g_hbm))
    ] + [pltpu.make_async_copy(gain_hbm, gain, in_sem.at[4])]
    for load in loads:
        load.start()
    lax.fori_loop(level + 1, levels, greet_later, 0)
    pl.semaphore_signal(barrier, inc=1, device_id=(seq, 1 - core), device_id_type=MESH)

    row = lax.broadcasted_iota(jnp.int32, (GROUP, GROUP), 0)
    col = lax.broadcasted_iota(jnp.int32, (GROUP, GROUP), 1)
    causal = col <= row
    sort = jnp.where(col == lax.rem(row, width) * heads + row // width, 1.0, 0.0).astype(BF16)
    unsort = jnp.where(col == lax.rem(row, heads) * width + row // heads, 1.0, 0.0).astype(BF16)

    def sorted_tiles(i):
        for tile in range(heads):
            yield tile, nn(sort, raw[i, pl.ds(tile * GROUP, GROUP), :])

    def put(dst, tile, value):
        for h in range(heads):
            dst[h, pl.ds(tile * width, width), :] = value[h * width : (h + 1) * width].astype(
                dst.dtype
            )

    def activate(i, act, slope):
        for tile, value in sorted_tiles(i):
            sigma = jax.nn.sigmoid(value)
            put(act, tile, value * sigma)
            put(slope, tile, sigma * (1.0 + value * (1.0 - sigma)))

    def store(i, out, head_value):
        values = [head_value(h).astype(BF16) for h in range(heads)]
        for tile in range(heads):
            piece = jnp.concatenate(
                [value[tile * width : (tile + 1) * width] for value in values], axis=0
            )
            results[i, pl.ds(tile * GROUP, GROUP), :] = nn(unsort, piece).astype(BF16)
        copy = pltpu.make_async_copy(results.at[i], out, out_sem.at[i])
        copy.start()
        return copy

    def bytes_of(ref, sem):
        return pltpu.make_async_copy(ref, ref, sem)

    others = pl.ds(0, PLANE - 1)

    def scatter(scan, chunk):
        def send(peer):
            pltpu.make_async_remote_copy(
                src_ref=own.at[scan, pl.ds(chunk * span + peer * rows, rows), :],
                dst_ref=gathered.at[scan, chunk, place],
                send_sem=send_sem.at[scan, 0, chunk],
                recv_sem=recv_sem.at[scan, 0, chunk],
                device_id=(level * PLANE + peer, core),
                device_id_type=MESH,
            ).start()

        each_peer(send)
        gathered[scan, chunk, place] = own[scan, pl.ds(chunk * span + place * rows, rows), :]

    def wait_scatter(scan, chunk):
        bytes_of(gathered.at[scan, chunk, others], recv_sem.at[scan, 0, chunk]).wait()

    def wait_scatter_send(scan, chunk):
        bytes_of(gathered.at[scan, chunk, others], send_sem.at[scan, 0, chunk]).wait()

    needing = ((level + 1, levels), (0, level))
    needed = ((0, level), (level + 1, levels))

    def z_copy(scan, chunk, target):
        return pltpu.make_async_remote_copy(
            src_ref=total.at[scan, chunk],
            dst_ref=z_slots.at[scan, chunk, level],
            send_sem=z_send_sem.at[scan, chunk, target],
            recv_sem=z_recv_sem.at[scan, chunk, level],
            device_id=(target * PLANE + place, core),
            device_id_type=MESH,
        )

    def own_total(scan, chunk):
        acc = gathered[scan, chunk, 0]
        for p in range(1, PLANE):
            acc = acc + gathered[scan, chunk, p]
        total[scan, chunk] = acc

        def send(target, carry):
            if scan == 0 and chunk == 0:
                pl.semaphore_wait(ready.at[target], 1)
            z_copy(scan, chunk, target).start()
            return carry

        lax.fori_loop(*needing[scan], send, 0)

    def all_prefixes(scan, chunk):
        def take(source, acc):
            bytes_of(z_slots.at[scan, chunk, source], z_recv_sem.at[scan, chunk, source]).wait()
            return acc + z_slots[scan, chunk, source]

        acc = lax.fori_loop(*needed[scan], take, jnp.zeros((rows, DH), F32))
        for p in range(PLANE) if scan == 0 else range(PLANE - 1, -1, -1):
            prefix[scan, chunk, p] = acc
            acc = acc + gathered[scan, chunk, p]

    def give_back(scan, chunk):
        def send(peer):
            pltpu.make_async_remote_copy(
                src_ref=prefix.at[scan, chunk, peer],
                dst_ref=state.at[scan, chunk, place],
                send_sem=send_sem.at[scan, 1, chunk],
                recv_sem=recv_sem.at[scan, 1, chunk],
                device_id=(level * PLANE + peer, core),
                device_id_type=MESH,
            ).start()

        if scan == 0:
            each_peer(send)
        else:

            @pl.when(place != 0)
            def _():
                send(0)

            def unless_first(peer):
                @pl.when(peer != 0)
                def _():
                    send(peer)

            each_peer(unless_first)
        state[scan, chunk, place] = prefix[scan, chunk, place]

    def wait_back(scan, chunk):
        bytes_of(state.at[scan, chunk, others], recv_sem.at[scan, 1, chunk]).wait()

    def drain(scan):
        for chunk in range(CHUNKS):
            wait_scatter_send(scan, chunk)
            bytes_of(state.at[scan, chunk, others], send_sem.at[scan, 1, chunk]).wait()

            def sent(target, carry):
                z_copy(scan, chunk, target).wait_send()
                return carry

            lax.fori_loop(*needing[scan], sent, 0)

    def middle(scan, work):
        for chunk in range(CHUNKS):
            wait_scatter(scan, chunk)
            own_total(scan, chunk)
        work()
        for chunk in range(CHUNKS):
            all_prefixes(scan, chunk)
            give_back(scan, chunk)

    def scanned(scan, h):
        chunk, at = h // per, h % per
        parts = PLANE // per
        return state[scan, chunk, pl.ds(at * parts, parts)].reshape(DH, DH).astype(BF16)

    loads[0].wait()
    activate(0, kact, kslope)
    loads[1].wait()
    for tile, value in sorted_tiles(1):
        put(vact, tile, value)
    for h in range(heads):
        own[0, pl.ds(h * DH, DH), :] = tn(kact[h], vact[h])

    pl.semaphore_wait(barrier, PLANE + level)
    lax.fori_loop(0, level, answer_earlier, 0)
    for chunk in range(CHUNKS):
        scatter(0, chunk)

    loads[2].wait()
    activate(2, qact, qslope)
    for h in range(heads):
        qact_t[h] = qact[h].T
        scores = nt(qact[h], kact[h])
        attn[h] = jnp.where(causal, scores, 0.0).astype(BF16)
        mixed[h] = nn(attn[h], vact[h])

    def weigh_grad():
        loads[3].wait()
        loads[4].wait()
        for tile, value in sorted_tiles(3):
            for h in range(heads):
                grad_in[h, pl.ds(tile * width, width), :] = (
                    value[h * width : (h + 1) * width] * gain[pl.ds(h, 1), :]
                )

    middle(0, weigh_grad)

    square = jnp.zeros((GROUP, DH), F32)
    crossed = jnp.zeros((GROUP, DH), F32)
    for h in range(heads):
        if h % per == 0:
            wait_back(0, h // per)
        state_b[h] = scanned(0, h)
        value = mixed[h] + nn(qact[h], state_b[h])
        mixed[h] = value
        square = square + value * value
        crossed = crossed + grad_in[h] * value
    square = jnp.sum(square, axis=1, keepdims=True)
    crossed = jnp.sum(crossed, axis=1, keepdims=True)
    lane = lax.broadcasted_iota(jnp.int32, (GROUP, DH), 1)
    stats[0] = jnp.where(lane == 0, square, jnp.where(lane == 1, crossed, 0.0))
    exchange = pltpu.make_async_remote_copy(
        src_ref=stats.at[0],
        dst_ref=stats.at[1],
        send_sem=stat_sem.at[0],
        recv_sem=stat_sem.at[1],
        device_id=(seq, 1 - core),
        device_id_type=MESH,
    )
    exchange.start()
    exchange.wait_recv()
    both = stats[1]
    features = heads * cores * DH
    square = square + both[:, 0:1]
    crossed = crossed + both[:, 1:2]
    inv_rms = lax.rsqrt(square * (1.0 / features) + 1e-06)
    factor = crossed * (inv_rms * inv_rms * inv_rms) * (1.0 / features)
    for h in range(heads):
        delta[h] = (grad_in[h] * inv_rms - mixed[h] * factor).astype(BF16)
        own[1, pl.ds(h * DH, DH), :] = nn(qact_t[h], delta[h])
        if (h + 1) % per == 0:
            scatter(1, h // per)

    copies = [store(0, normed_out, lambda h: mixed[h] * inv_rms * gain[pl.ds(h, 1), :])]

    def local_grads(some_heads):
        for h in some_heads:
            bscore = jnp.where(causal, nt(delta[h], vact[h]), 0.0).astype(BF16)
            mixed[h] = (nn(bscore, kact[h]) + nt(delta[h], state_b[h])) * qslope[h]
            dk[h] = tn(bscore, qact[h])
            dv[h] = tn(attn[h], delta[h])

    local_grads(range(heads // 2))
    middle(1, lambda: None)
    local_grads(range(heads // 2, heads))
    copies.append(store(1, qg_out, lambda h: mixed[h]))
    exchange.wait_send()
    drain(0)

    for h in range(heads):
        if h % per == 0:
            wait_back(1, h // per)
        state_b[h] = scanned(1, h)
        dk[h] = (dk[h] + nt(vact[h], state_b[h])) * kslope[h]
        dv[h] = dv[h] + nn(kact[h], state_b[h])
    copies.append(store(2, kg_out, lambda h: dk[h]))
    copies.append(store(3, vg_out, lambda h: dv[h]))
    drain(1)
    for copy in copies:
        copy.wait()


def deliver(*refs):
    count = len(refs) // 2
    sems = refs[-1]
    copies = [
        pltpu.make_async_copy(refs[i], refs[count + i], sems.at[i]) for i in range(count)
    ]
    for copy in copies:
        copy.start()
    for copy in copies:
        copy.wait()


def body(query_raw, key_raw, value_raw, out_gain, out_grad):
    tokens, heads, width = query_raw.shape
    levels = lax.axis_size("seq") // PLANE
    cores = lax.axis_size("head")
    flat = (tokens * heads, width)
    rows = heads * DH // (CHUNKS * PLANE)
    anywhere = pl.BlockSpec(memory_space=pl.ANY)
    in_hbm = pl.BlockSpec(memory_space=pltpu.HBM)
    per_head = (heads, GROUP, DH)
    dma = pltpu.SemaphoreType.DMA
    outs = pl.pallas_call(
        functools.partial(kernel, levels, heads, cores),
        out_shape=[pltpu.VMEM(flat, BF16)] * 4,
        in_specs=[in_hbm] * 5,
        out_specs=[anywhere] * 4,
        scratch_shapes=[
            pltpu.VMEM((4,) + flat, BF16),
            pltpu.VMEM((4,) + flat, BF16),
            pltpu.VMEM((heads, DH), F32),
            pltpu.VMEM(per_head, BF16),
            pltpu.VMEM((heads, DH, GROUP), BF16),
            pltpu.VMEM(per_head, BF16),
            pltpu.VMEM(per_head, BF16),
            pltpu.VMEM(per_head, F32),
            pltpu.VMEM(per_head, F32),
            pltpu.VMEM(per_head, F32),
            pltpu.VMEM((heads, GROUP, GROUP), BF16),
            pltpu.VMEM(per_head, F32),
            pltpu.VMEM(per_head, BF16),
            pltpu.VMEM(per_head, F32),
            pltpu.VMEM(per_head, F32),
            pltpu.VMEM((heads, DH, DH), BF16),
            pltpu.VMEM((2, heads * DH, DH), F32),
            pltpu.VMEM((2, CHUNKS, PLANE, rows, DH), F32),
            pltpu.VMEM((2, CHUNKS, PLANE, rows, DH), F32),
            pltpu.VMEM((2, CHUNKS, rows, DH), F32),
            pltpu.VMEM((2, CHUNKS, levels, rows, DH), F32),
            pltpu.VMEM((2, CHUNKS, PLANE, rows, DH), F32),
            pltpu.VMEM((2, GROUP, DH), F32),
            dma((5,)),
            dma((2, 2, CHUNKS)),
            dma((2, 2, CHUNKS)),
            dma((2, CHUNKS, levels)),
            dma((2, CHUNKS, levels)),
            dma((2,)),
            dma((4,)),
            pltpu.SemaphoreType.REGULAR((levels,)),
        ],
        compiler_params=pltpu.CompilerParams(
            collective_id=0, has_side_effects=True, vmem_limit_bytes=60 * 1024 * 1024
        ),
    )(
        query_raw.reshape(flat),
        key_raw.reshape(flat),
        value_raw.reshape(flat),
        out_gain,
        out_grad.reshape(flat),
    )
    outs = pl.pallas_call(
        deliver,
        out_shape=[pltpu.HBM(flat, BF16)] * 4,
        in_specs=[anywhere] * 4,
        out_specs=[in_hbm] * 4,
        scratch_shapes=[dma((4,))],
        compiler_params=pltpu.CompilerParams(vmem_limit_bytes=4 * 1024 * 1024),
    )(*outs)
    return tuple(out.reshape(tokens, heads, width) for out in outs)


def solution(mesh):
    rows = P("seq", "head", None)
    return jax.shard_map(
        body,
        mesh=mesh,
        in_specs=(rows, rows, rows, P("head", None), rows),
        out_specs=(rows,) * 4,
        check_vma=False,
    )
```

```python
import functools

import jax
import jax.numpy as jnp
from jax import lax
from jax.experimental import pallas as pl
from jax.experimental.pallas import tpu as pltpu
from jax.sharding import PartitionSpec as P

GROUP = 256
DH = 128
WIDE, LONG = 4, 8
PLANE = WIDE * LONG
RELAY = 3
CHUNKS = 2
MESH = pl.DeviceIdType.MESH
F32 = jnp.float32
BF16 = jnp.bfloat16


def dot(lhs, rhs, contract):
    return lax.dot_general(lhs, rhs, (contract, ((), ())), preferred_element_type=F32)


def nn(lhs, rhs):
    return dot(lhs, rhs, ((1,), (0,)))


def nt(lhs, rhs):
    return dot(lhs, rhs, ((1,), (1,)))


def tn(lhs, rhs):
    return dot(lhs, rhs, ((0,), (0,)))


def kernel(
    levels,
    heads,
    cores,
    q_hbm,
    k_hbm,
    v_hbm,
    gain_hbm,
    g_hbm,
    normed_out,
    qg_out,
    kg_out,
    vg_out,
    raw,
    results,
    gain,
    qact,
    qact_t,
    kact,
    vact,
    qslope,
    kslope,
    grad_in,
    attn,
    mixed,
    delta,
    dk,
    dv,
    state_b,
    own,
    gathered,
    prefix,
    total,
    z_slots,
    state,
    stats,
    in_sem,
    send_sem,
    recv_sem,
    z_send_sem,
    z_recv_sem,
    stat_sem,
    out_sem,
    ready,
    relay_sem,
):
    seq = lax.axis_index("seq")
    core = lax.axis_index("head")
    level = seq // PLANE
    place = lax.rem(seq, PLANE)
    rows = heads * DH // (CHUNKS * PLANE)
    span = heads * DH // CHUNKS
    per = heads // CHUNKS
    width = GROUP // heads

    across, along = place // LONG, lax.rem(place, LONG)

    def each_peer(act):
        half = LONG // 2
        steps = [half]
        for off in range(1, half):
            steps += [half - off, half + off]

        for step in steps + [0]:

            def one(turn, carry, step=step):
                x = lax.rem(across + lax.rem(turn + WIDE // 2, WIDE), WIDE)
                act(x * LONG + lax.rem(along + step, LONG))
                return carry

            if step:
                lax.fori_loop(0, WIDE, one, 0)
            else:
                lax.fori_loop(0, WIDE // 2, one, 0)
                lax.fori_loop(WIDE // 2 + 1, WIDE, one, 0)

    barrier = pltpu.get_barrier_semaphore()

    def greet(peer):
        pl.semaphore_signal(
            barrier, inc=1, device_id=(level * PLANE + peer, core), device_id_type=MESH
        )

    def greet_later(other, carry):
        pl.semaphore_signal(
            barrier, inc=1, device_id=(other * PLANE + place, core), device_id_type=MESH
        )
        return carry

    def answer_earlier(other, carry):
        pl.semaphore_signal(
            ready.at[level], inc=1, device_id=(other * PLANE + place, core), device_id_type=MESH
        )
        return carry

    each_peer(greet)
    loads = [
        pltpu.make_async_copy(hbm, raw.at[i], in_sem.at[i])
        for i, hbm in enumerate((k_hbm, v_hbm, q_hbm, g_hbm))
    ] + [pltpu.make_async_copy(gain_hbm, gain, in_sem.at[4])]
    for load in loads:
        load.start()
    lax.fori_loop(level + 1, levels, greet_later, 0)
    pl.semaphore_signal(barrier, inc=1, device_id=(seq, 1 - core), device_id_type=MESH)

    row = lax.broadcasted_iota(jnp.int32, (GROUP, GROUP), 0)
    col = lax.broadcasted_iota(jnp.int32, (GROUP, GROUP), 1)
    causal = col <= row
    sort = jnp.where(col == lax.rem(row, width) * heads + row // width, 1.0, 0.0).astype(BF16)
    unsort = jnp.where(col == lax.rem(row, heads) * width + row // heads, 1.0, 0.0).astype(BF16)

    def sorted_tiles(i):
        for tile in range(heads):
            yield tile, nn(sort, raw[i, pl.ds(tile * GROUP, GROUP), :])

    def put(dst, tile, value):
        for h in range(heads):
            dst[h, pl.ds(tile * width, width), :] = value[h * width : (h + 1) * width].astype(
                dst.dtype
            )

    def activate(i, act, slope):
        for tile, value in sorted_tiles(i):
            sigma = jax.nn.sigmoid(value)
            put(act, tile, value * sigma)
            put(slope, tile, sigma * (1.0 + value * (1.0 - sigma)))

    def store(i, out, head_value):
        values = [head_value(h).astype(BF16) for h in range(heads)]
        for tile in range(heads):
            piece = jnp.concatenate(
                [value[tile * width : (tile + 1) * width] for value in values], axis=0
            )
            results[i, pl.ds(tile * GROUP, GROUP), :] = nn(unsort, piece).astype(BF16)
        copy = pltpu.make_async_copy(results.at[i], out, out_sem.at[i])
        copy.start()
        return copy

    def bytes_of(ref, sem):
        return pltpu.make_async_copy(ref, ref, sem)

    others = pl.ds(0, PLANE - 1)

    def scatter(scan, chunk):
        def send(peer):
            pltpu.make_async_remote_copy(
                src_ref=own.at[scan, pl.ds(chunk * span + peer * rows, rows), :],
                dst_ref=gathered.at[scan, chunk, place],
                send_sem=send_sem.at[scan, 0, chunk],
                recv_sem=recv_sem.at[scan, 0, chunk],
                device_id=(level * PLANE + peer, core),
                device_id_type=MESH,
            ).start()

        each_peer(send)
        gathered[scan, chunk, place] = own[scan, pl.ds(chunk * span + place * rows, rows), :]

    def wait_scatter(scan, chunk):
        bytes_of(gathered.at[scan, chunk, others], recv_sem.at[scan, 0, chunk]).wait()

    def wait_scatter_send(scan, chunk):
        bytes_of(gathered.at[scan, chunk, others], send_sem.at[scan, 0, chunk]).wait()

    needing = ((level + 1, levels), (0, level))
    needed = ((0, level), (level + 1, levels))

    def z_copy(scan, chunk, target):
        return pltpu.make_async_remote_copy(
            src_ref=total.at[scan, chunk],
            dst_ref=z_slots.at[scan, chunk, level],
            send_sem=z_send_sem.at[scan, chunk, target],
            recv_sem=z_recv_sem.at[scan, chunk, level],
            device_id=(target * PLANE + place, core),
            device_id_type=MESH,
        )

    def own_total(scan, chunk):
        acc = gathered[scan, chunk, 0]
        for p in range(1, PLANE):
            acc = acc + gathered[scan, chunk, p]
        total[scan, chunk] = acc

        def send(target, carry):
            if scan == 0 and chunk == 0:
                pl.semaphore_wait(ready.at[target], 1)
            if scan == 0:

                @pl.when(target - level != 2 * RELAY)
                def _():
                    z_copy(scan, chunk, target).start()
            else:
                z_copy(scan, chunk, target).start()
            return carry

        lax.fori_loop(*needing[scan], send, 0)

    relays = jnp.logical_and(level >= RELAY, level + RELAY < levels)

    def relay_copy(chunk):
        slot = lax.rem(level + levels - RELAY, levels)
        target = lax.rem(level + RELAY, levels)
        return pltpu.make_async_remote_copy(
            src_ref=z_slots.at[0, chunk, slot],
            dst_ref=z_slots.at[0, chunk, slot],
            send_sem=relay_sem.at[chunk],
            recv_sem=z_recv_sem.at[0, chunk, slot],
            device_id=(target * PLANE + place, core),
            device_id_type=MESH,
        )

    def pass_on(chunk):
        @pl.when(relays)
        def _():
            relay_copy(chunk).start()

    def all_prefixes(scan, chunk):
        def take(source, acc):
            bytes_of(z_slots.at[scan, chunk, source], z_recv_sem.at[scan, chunk, source]).wait()
            return acc + z_slots[scan, chunk, source]

        acc = jnp.zeros((rows, DH), F32)
        if scan == 0:
            middle = jnp.maximum(level - RELAY, 0)
            acc = lax.fori_loop(middle, jnp.minimum(middle + 1, level), take, acc)
            pass_on(chunk)
            acc = lax.fori_loop(0, middle, take, acc)
            acc = lax.fori_loop(middle + 1, level, take, acc)
        else:
            acc = lax.fori_loop(*needed[scan], take, acc)
        for p in range(PLANE) if scan == 0 else range(PLANE - 1, -1, -1):
            prefix[scan, chunk, p] = acc
            acc = acc + gathered[scan, chunk, p]

    def give_back(scan, chunk):
        def send(peer):
            pltpu.make_async_remote_copy(
                src_ref=prefix.at[scan, chunk, peer],
                dst_ref=state.at[scan, chunk, place],
                send_sem=send_sem.at[scan, 1, chunk],
                recv_sem=recv_sem.at[scan, 1, chunk],
                device_id=(level * PLANE + peer, core),
                device_id_type=MESH,
            ).start()

        if scan == 0:
            each_peer(send)
        else:

            @pl.when(place != 0)
            def _():
                send(0)

            def unless_first(peer):
                @pl.when(peer != 0)
                def _():
                    send(peer)

            each_peer(unless_first)
        state[scan, chunk, place] = prefix[scan, chunk, place]

    def wait_back(scan, chunk):
        bytes_of(state.at[scan, chunk, others], recv_sem.at[scan, 1, chunk]).wait()

    def drain(scan):
        for chunk in range(CHUNKS):
            wait_scatter_send(scan, chunk)
            bytes_of(state.at[scan, chunk, others], send_sem.at[scan, 1, chunk]).wait()

            def sent(target, carry):
                if scan == 0:

                    @pl.when(target - level != 2 * RELAY)
                    def _():
                        z_copy(scan, chunk, target).wait_send()
                else:
                    z_copy(scan, chunk, target).wait_send()
                return carry

            lax.fori_loop(*needing[scan], sent, 0)
            if scan == 0:

                @pl.when(relays)
                def _():
                    relay_copy(chunk).wait_send()

    def middle(scan, work):
        for chunk in range(CHUNKS):
            wait_scatter(scan, chunk)
            own_total(scan, chunk)
        work()
        for chunk in range(CHUNKS):
            all_prefixes(scan, chunk)
            give_back(scan, chunk)

    def scanned(scan, h):
        chunk, at = h // per, h % per
        parts = PLANE // per
        return state[scan, chunk, pl.ds(at * parts, parts)].reshape(DH, DH).astype(BF16)

    loads[0].wait()
    activate(0, kact, kslope)
    loads[1].wait()
    for tile, value in sorted_tiles(1):
        put(vact, tile, value)
    for h in range(heads):
        own[0, pl.ds(h * DH, DH), :] = tn(kact[h], vact[h])

    pl.semaphore_wait(barrier, PLANE + level)
    lax.fori_loop(0, level, answer_earlier, 0)
    for chunk in range(CHUNKS):
        scatter(0, chunk)

    loads[2].wait()
    activate(2, qact, qslope)
    for h in range(heads):
        qact_t[h] = qact[h].T
        scores = nt(qact[h], kact[h])
        attn[h] = jnp.where(causal, scores, 0.0).astype(BF16)
        mixed[h] = nn(attn[h], vact[h])

    def weigh_grad():
        loads[3].wait()
        loads[4].wait()
        for tile, value in sorted_tiles(3):
            for h in range(heads):
                grad_in[h, pl.ds(tile * width, width), :] = (
                    value[h * width : (h + 1) * width] * gain[pl.ds(h, 1), :]
                )

    middle(0, weigh_grad)

    square = jnp.zeros((GROUP, DH), F32)
    crossed = jnp.zeros((GROUP, DH), F32)
    for h in range(heads):
        if h % per == 0:
            wait_back(0, h // per)
        state_b[h] = scanned(0, h)
        value = mixed[h] + nn(qact[h], state_b[h])
        mixed[h] = value
        square = square + value * value
        crossed = crossed + grad_in[h] * value
    square = jnp.sum(square, axis=1, keepdims=True)
    crossed = jnp.sum(crossed, axis=1, keepdims=True)
    lane = lax.broadcasted_iota(jnp.int32, (GROUP, DH), 1)
    stats[0] = jnp.where(lane == 0, square, jnp.where(lane == 1, crossed, 0.0))
    exchange = pltpu.make_async_remote_copy(
        src_ref=stats.at[0],
        dst_ref=stats.at[1],
        send_sem=stat_sem.at[0],
        recv_sem=stat_sem.at[1],
        device_id=(seq, 1 - core),
        device_id_type=MESH,
    )
    exchange.start()
    exchange.wait_recv()
    both = stats[1]
    features = heads * cores * DH
    square = square + both[:, 0:1]
    crossed = crossed + both[:, 1:2]
    inv_rms = lax.rsqrt(square * (1.0 / features) + 1e-06)
    factor = crossed * (inv_rms * inv_rms * inv_rms) * (1.0 / features)
    for h in range(heads):
        delta[h] = (grad_in[h] * inv_rms - mixed[h] * factor).astype(BF16)
        own[1, pl.ds(h * DH, DH), :] = nn(qact_t[h], delta[h])
        if (h + 1) % per == 0:
            scatter(1, h // per)

    copies = [store(0, normed_out, lambda h: mixed[h] * inv_rms * gain[pl.ds(h, 1), :])]

    def local_grads(some_heads):
        for h in some_heads:
            bscore = jnp.where(causal, nt(delta[h], vact[h]), 0.0).astype(BF16)
            mixed[h] = (nn(bscore, kact[h]) + nt(delta[h], state_b[h])) * qslope[h]
            dk[h] = tn(bscore, qact[h])
            dv[h] = tn(attn[h], delta[h])

    local_grads(range(heads // 2))
    middle(1, lambda: None)
    local_grads(range(heads // 2, heads))
    copies.append(store(1, qg_out, lambda h: mixed[h]))
    exchange.wait_send()
    drain(0)

    for h in range(heads):
        if h % per == 0:
            wait_back(1, h // per)
        state_b[h] = scanned(1, h)
        dk[h] = (dk[h] + nt(vact[h], state_b[h])) * kslope[h]
        dv[h] = dv[h] + nn(kact[h], state_b[h])
    copies.append(store(2, kg_out, lambda h: dk[h]))
    copies.append(store(3, vg_out, lambda h: dv[h]))
    drain(1)
    for copy in copies:
        copy.wait()


def deliver(*refs):
    count = len(refs) // 2
    sems = refs[-1]
    copies = [
        pltpu.make_async_copy(refs[i], refs[count + i], sems.at[i]) for i in range(count)
    ]
    for copy in copies:
        copy.start()
    for copy in copies:
        copy.wait()


def body(query_raw, key_raw, value_raw, out_gain, out_grad):
    tokens, heads, width = query_raw.shape
    levels = lax.axis_size("seq") // PLANE
    cores = lax.axis_size("head")
    flat = (tokens * heads, width)
    rows = heads * DH // (CHUNKS * PLANE)
    anywhere = pl.BlockSpec(memory_space=pl.ANY)
    in_hbm = pl.BlockSpec(memory_space=pltpu.HBM)
    per_head = (heads, GROUP, DH)
    dma = pltpu.SemaphoreType.DMA
    outs = pl.pallas_call(
        functools.partial(kernel, levels, heads, cores),
        out_shape=[pltpu.VMEM(flat, BF16)] * 4,
        in_specs=[in_hbm] * 5,
        out_specs=[anywhere] * 4,
        scratch_shapes=[
            pltpu.VMEM((4,) + flat, BF16),
            pltpu.VMEM((4,) + flat, BF16),
            pltpu.VMEM((heads, DH), F32),
            pltpu.VMEM(per_head, BF16),
            pltpu.VMEM((heads, DH, GROUP), BF16),
            pltpu.VMEM(per_head, BF16),
            pltpu.VMEM(per_head, BF16),
            pltpu.VMEM(per_head, F32),
            pltpu.VMEM(per_head, F32),
            pltpu.VMEM(per_head, F32),
            pltpu.VMEM((heads, GROUP, GROUP), BF16),
            pltpu.VMEM(per_head, F32),
            pltpu.VMEM(per_head, BF16),
            pltpu.VMEM(per_head, F32),
            pltpu.VMEM(per_head, F32),
            pltpu.VMEM((heads, DH, DH), BF16),
            pltpu.VMEM((2, heads * DH, DH), F32),
            pltpu.VMEM((2, CHUNKS, PLANE, rows, DH), F32),
            pltpu.VMEM((2, CHUNKS, PLANE, rows, DH), F32),
            pltpu.VMEM((2, CHUNKS, rows, DH), F32),
            pltpu.VMEM((2, CHUNKS, levels, rows, DH), F32),
            pltpu.VMEM((2, CHUNKS, PLANE, rows, DH), F32),
            pltpu.VMEM((2, GROUP, DH), F32),
            dma((5,)),
            dma((2, 2, CHUNKS)),
            dma((2, 2, CHUNKS)),
            dma((2, CHUNKS, levels)),
            dma((2, CHUNKS, levels)),
            dma((2,)),
            dma((4,)),
            pltpu.SemaphoreType.REGULAR((levels,)),
            dma((CHUNKS,)),
        ],
        compiler_params=pltpu.CompilerParams(
            collective_id=0, has_side_effects=True, vmem_limit_bytes=60 * 1024 * 1024
        ),
    )(
        query_raw.reshape(flat),
        key_raw.reshape(flat),
        value_raw.reshape(flat),
        out_gain,
        out_grad.reshape(flat),
    )
    outs = pl.pallas_call(
        deliver,
        out_shape=[pltpu.HBM(flat, BF16)] * 4,
        in_specs=[anywhere] * 4,
        out_specs=[in_hbm] * 4,
        scratch_shapes=[dma((4,))],
        compiler_params=pltpu.CompilerParams(vmem_limit_bytes=4 * 1024 * 1024),
    )(*outs)
    return tuple(out.reshape(tokens, heads, width) for out in outs)


def solution(mesh):
    rows = P("seq", "head", None)
    return jax.shard_map(
        body,
        mesh=mesh,
        in_specs=(rows, rows, rows, P("head", None), rows),
        out_specs=(rows,) * 4,
        check_vma=False,
    )
```

```python
import functools

import jax
import jax.numpy as jnp
from jax import lax
from jax.experimental import pallas as pl
from jax.experimental.pallas import tpu as pltpu
from jax.sharding import PartitionSpec as P

GROUP = 256
DH = 128
WIDE, LONG = 4, 8
PLANE = WIDE * LONG
CHUNKS = (1, 2)
MESH = pl.DeviceIdType.MESH
F32 = jnp.float32
BF16 = jnp.bfloat16


def dot(lhs, rhs, contract):
    return lax.dot_general(lhs, rhs, (contract, ((), ())), preferred_element_type=F32)


def nn(lhs, rhs):
    return dot(lhs, rhs, ((1,), (0,)))


def nt(lhs, rhs):
    return dot(lhs, rhs, ((1,), (1,)))


def tn(lhs, rhs):
    return dot(lhs, rhs, ((0,), (0,)))


def kernel(
    levels,
    heads,
    cores,
    q_hbm,
    k_hbm,
    v_hbm,
    gain_hbm,
    g_hbm,
    normed_out,
    qg_out,
    kg_out,
    vg_out,
    raw,
    results,
    gain,
    qact,
    qact_t,
    kact,
    vact,
    qslope,
    kslope,
    grad_in,
    attn,
    mixed,
    delta,
    dk,
    dv,
    state_b,
    own,
    gathered,
    prefix,
    total,
    z_slots,
    state,
    stats,
    in_sem,
    send_sem,
    recv_sem,
    z_send_sem,
    z_recv_sem,
    stat_sem,
    out_sem,
    ready,
):
    seq = lax.axis_index("seq")
    core = lax.axis_index("head")
    level = seq // PLANE
    place = lax.rem(seq, PLANE)
    rows = [heads * DH // (count * PLANE) for count in CHUNKS]
    span = [heads * DH // count for count in CHUNKS]
    per = [heads // count for count in CHUNKS]
    width = GROUP // heads

    across, along = place // LONG, lax.rem(place, LONG)

    def each_peer(act):
        half = LONG // 2
        steps = [half]
        for off in range(1, half):
            steps += [half - off, half + off]

        for step in steps + [0]:

            def one(turn, carry, step=step):
                x = lax.rem(across + lax.rem(turn + WIDE // 2, WIDE), WIDE)
                act(x * LONG + lax.rem(along + step, LONG))
                return carry

            if step:
                lax.fori_loop(0, WIDE, one, 0)
            else:
                lax.fori_loop(0, WIDE // 2, one, 0)
                lax.fori_loop(WIDE // 2 + 1, WIDE, one, 0)

    barrier = pltpu.get_barrier_semaphore()

    def greet(peer):
        pl.semaphore_signal(
            barrier, inc=1, device_id=(level * PLANE + peer, core), device_id_type=MESH
        )

    def greet_later(other, carry):
        pl.semaphore_signal(
            barrier, inc=1, device_id=(other * PLANE + place, core), device_id_type=MESH
        )
        return carry

    def answer_earlier(other, carry):
        pl.semaphore_signal(
            ready.at[level], inc=1, device_id=(other * PLANE + place, core), device_id_type=MESH
        )
        return carry

    each_peer(greet)
    loads = [
        pltpu.make_async_copy(hbm, raw.at[i], in_sem.at[i])
        for i, hbm in enumerate((k_hbm, v_hbm, q_hbm, g_hbm))
    ] + [pltpu.make_async_copy(gain_hbm, gain, in_sem.at[4])]
    for load in loads:
        load.start()
    lax.fori_loop(level + 1, levels, greet_later, 0)
    pl.semaphore_signal(barrier, inc=1, device_id=(seq, 1 - core), device_id_type=MESH)

    row = lax.broadcasted_iota(jnp.int32, (GROUP, GROUP), 0)
    col = lax.broadcasted_iota(jnp.int32, (GROUP, GROUP), 1)
    causal = col <= row
    sort = jnp.where(col == lax.rem(row, width) * heads + row // width, 1.0, 0.0).astype(BF16)
    unsort = jnp.where(col == lax.rem(row, heads) * width + row // heads, 1.0, 0.0).astype(BF16)

    def sorted_tiles(i):
        for tile in range(heads):
            yield tile, nn(sort, raw[i, pl.ds(tile * GROUP, GROUP), :])

    def put(dst, tile, value):
        for h in range(heads):
            dst[h, pl.ds(tile * width, width), :] = value[h * width : (h + 1) * width].astype(
                dst.dtype
            )

    def activate(i, act, slope):
        for tile, value in sorted_tiles(i):
            sigma = jax.nn.sigmoid(value)
            put(act, tile, value * sigma)
            put(slope, tile, sigma * (1.0 + value * (1.0 - sigma)))

    def store(i, out, head_value):
        values = [head_value(h).astype(BF16) for h in range(heads)]
        for tile in range(heads):
            piece = jnp.concatenate(
                [value[tile * width : (tile + 1) * width] for value in values], axis=0
            )
            results[i, pl.ds(tile * GROUP, GROUP), :] = nn(unsort, piece).astype(BF16)
        copy = pltpu.make_async_copy(results.at[i], out, out_sem.at[i])
        copy.start()
        return copy

    def bytes_of(ref, sem):
        return pltpu.make_async_copy(ref, ref, sem)

    others = pl.ds(0, PLANE - 1)

    def scatter(scan, chunk):
        def send(peer):
            pltpu.make_async_remote_copy(
                src_ref=own.at[scan, pl.ds(chunk * span[scan] + peer * rows[scan], rows[scan]), :],
                dst_ref=gathered[scan].at[chunk, place],
                send_sem=send_sem.at[scan, 0, chunk],
                recv_sem=recv_sem.at[scan, 0, chunk],
                device_id=(level * PLANE + peer, core),
                device_id_type=MESH,
            ).start()

        each_peer(send)
        gathered[scan][chunk, place] = own[
            scan, pl.ds(chunk * span[scan] + place * rows[scan], rows[scan]), :
        ]

    def wait_scatter(scan, chunk):
        bytes_of(gathered[scan].at[chunk, others], recv_sem.at[scan, 0, chunk]).wait()

    def wait_scatter_send(scan, chunk):
        bytes_of(gathered[scan].at[chunk, others], send_sem.at[scan, 0, chunk]).wait()

    needing = ((level + 1, levels), (0, level))
    needed = ((0, level), (level + 1, levels))

    def z_copy(scan, chunk, target):
        return pltpu.make_async_remote_copy(
            src_ref=total[scan].at[chunk],
            dst_ref=z_slots[scan].at[chunk, level],
            send_sem=z_send_sem.at[scan, chunk, target],
            recv_sem=z_recv_sem.at[scan, chunk, level],
            device_id=(target * PLANE + place, core),
            device_id_type=MESH,
        )

    def own_total(scan, chunk):
        acc = gathered[scan][chunk, 0]
        for p in range(1, PLANE):
            acc = acc + gathered[scan][chunk, p]
        total[scan][chunk] = acc

        def send(target, carry):
            if scan == 0 and chunk == 0:
                pl.semaphore_wait(ready.at[target], 1)
            z_copy(scan, chunk, target).start()
            return carry

        lax.fori_loop(*needing[scan], send, 0)

    def all_prefixes(scan, chunk):
        def take(source, acc):
            bytes_of(z_slots[scan].at[chunk, source], z_recv_sem.at[scan, chunk, source]).wait()
            return acc + z_slots[scan][chunk, source]

        acc = lax.fori_loop(*needed[scan], take, jnp.zeros((rows[scan], DH), F32))
        for p in range(PLANE) if scan == 0 else range(PLANE - 1, -1, -1):
            prefix[scan][chunk, p] = acc
            acc = acc + gathered[scan][chunk, p]

    def give_back(scan, chunk):
        def send(peer):
            pltpu.make_async_remote_copy(
                src_ref=prefix[scan].at[chunk, peer],
                dst_ref=state[scan].at[chunk, place],
                send_sem=send_sem.at[scan, 1, chunk],
                recv_sem=recv_sem.at[scan, 1, chunk],
                device_id=(level * PLANE + peer, core),
                device_id_type=MESH,
            ).start()

        if scan == 0:
            each_peer(send)
        else:

            @pl.when(place != 0)
            def _():
                send(0)

            def unless_first(peer):
                @pl.when(peer != 0)
                def _():
                    send(peer)

            each_peer(unless_first)
        state[scan][chunk, place] = prefix[scan][chunk, place]

    def wait_back(scan, chunk):
        bytes_of(state[scan].at[chunk, others], recv_sem.at[scan, 1, chunk]).wait()

    def drain(scan):
        for chunk in range(CHUNKS[scan]):
            wait_scatter_send(scan, chunk)
            bytes_of(state[scan].at[chunk, others], send_sem.at[scan, 1, chunk]).wait()

            def sent(target, carry):
                z_copy(scan, chunk, target).wait_send()
                return carry

            lax.fori_loop(*needing[scan], sent, 0)

    def middle(scan, work):
        for chunk in range(CHUNKS[scan]):
            wait_scatter(scan, chunk)
            own_total(scan, chunk)
        work()
        for chunk in range(CHUNKS[scan]):
            all_prefixes(scan, chunk)
            give_back(scan, chunk)

    def scanned(scan, h):
        chunk, at = h // per[scan], h % per[scan]
        parts = PLANE // per[scan]
        return state[scan][chunk, pl.ds(at * parts, parts)].reshape(DH, DH).astype(BF16)

    loads[0].wait()
    activate(0, kact, kslope)
    loads[1].wait()
    for tile, value in sorted_tiles(1):
        put(vact, tile, value)
    for h in range(heads):
        own[0, pl.ds(h * DH, DH), :] = tn(kact[h], vact[h])

    pl.semaphore_wait(barrier, PLANE + level)
    lax.fori_loop(0, level, answer_earlier, 0)
    for chunk in range(CHUNKS[0]):
        scatter(0, chunk)

    loads[2].wait()
    activate(2, qact, qslope)
    for h in range(heads):
        qact_t[h] = qact[h].T
        scores = nt(qact[h], kact[h])
        attn[h] = jnp.where(causal, scores, 0.0).astype(BF16)
        mixed[h] = nn(attn[h], vact[h])

    def weigh_grad():
        loads[3].wait()
        loads[4].wait()
        for tile, value in sorted_tiles(3):
            for h in range(heads):
                grad_in[h, pl.ds(tile * width, width), :] = (
                    value[h * width : (h + 1) * width] * gain[pl.ds(h, 1), :]
                )

    middle(0, weigh_grad)

    square = jnp.zeros((GROUP, DH), F32)
    crossed = jnp.zeros((GROUP, DH), F32)
    for h in range(heads):
        if h % per[0] == 0:
            wait_back(0, h // per[0])
        state_b[h] = scanned(0, h)
        value = mixed[h] + nn(qact[h], state_b[h])
        mixed[h] = value
        square = square + value * value
        crossed = crossed + grad_in[h] * value
    square = jnp.sum(square, axis=1, keepdims=True)
    crossed = jnp.sum(crossed, axis=1, keepdims=True)
    lane = lax.broadcasted_iota(jnp.int32, (GROUP, DH), 1)
    stats[0] = jnp.where(lane == 0, square, jnp.where(lane == 1, crossed, 0.0))
    exchange = pltpu.make_async_remote_copy(
        src_ref=stats.at[0],
        dst_ref=stats.at[1],
        send_sem=stat_sem.at[0],
        recv_sem=stat_sem.at[1],
        device_id=(seq, 1 - core),
        device_id_type=MESH,
    )
    exchange.start()
    exchange.wait_recv()
    both = stats[1]
    features = heads * cores * DH
    square = square + both[:, 0:1]
    crossed = crossed + both[:, 1:2]
    inv_rms = lax.rsqrt(square * (1.0 / features) + 1e-06)
    factor = crossed * (inv_rms * inv_rms * inv_rms) * (1.0 / features)
    for h in range(heads):
        delta[h] = (grad_in[h] * inv_rms - mixed[h] * factor).astype(BF16)
        own[1, pl.ds(h * DH, DH), :] = nn(qact_t[h], delta[h])
        if (h + 1) % per[1] == 0:
            scatter(1, h // per[1])

    copies = [store(0, normed_out, lambda h: mixed[h] * inv_rms * gain[pl.ds(h, 1), :])]

    def local_grads(some_heads):
        for h in some_heads:
            bscore = jnp.where(causal, nt(delta[h], vact[h]), 0.0).astype(BF16)
            mixed[h] = (nn(bscore, kact[h]) + nt(delta[h], state_b[h])) * qslope[h]
            dk[h] = tn(bscore, qact[h])
            dv[h] = tn(attn[h], delta[h])

    local_grads(range(heads // 2))
    middle(1, lambda: None)
    local_grads(range(heads // 2, heads))
    copies.append(store(1, qg_out, lambda h: mixed[h]))
    exchange.wait_send()
    drain(0)

    for h in range(heads):
        if h % per[1] == 0:
            wait_back(1, h // per[1])
        state_b[h] = scanned(1, h)
        dk[h] = (dk[h] + nt(vact[h], state_b[h])) * kslope[h]
        dv[h] = dv[h] + nn(kact[h], state_b[h])
    copies.append(store(2, kg_out, lambda h: dk[h]))
    copies.append(store(3, vg_out, lambda h: dv[h]))
    drain(1)
    for copy in copies:
        copy.wait()


def deliver(*refs):
    count = len(refs) // 2
    sems = refs[-1]
    copies = [
        pltpu.make_async_copy(refs[i], refs[count + i], sems.at[i]) for i in range(count)
    ]
    for copy in copies:
        copy.start()
    for copy in copies:
        copy.wait()


def body(query_raw, key_raw, value_raw, out_gain, out_grad):
    tokens, heads, width = query_raw.shape
    levels = lax.axis_size("seq") // PLANE
    cores = lax.axis_size("head")
    flat = (tokens * heads, width)
    most = max(CHUNKS)

    def per_scan(*slots):
        return [
            pltpu.VMEM((count,) + slots + (heads * DH // (count * PLANE), DH), F32)
            for count in CHUNKS
        ]

    anywhere = pl.BlockSpec(memory_space=pl.ANY)
    in_hbm = pl.BlockSpec(memory_space=pltpu.HBM)
    per_head = (heads, GROUP, DH)
    dma = pltpu.SemaphoreType.DMA
    outs = pl.pallas_call(
        functools.partial(kernel, levels, heads, cores),
        out_shape=[pltpu.VMEM(flat, BF16)] * 4,
        in_specs=[in_hbm] * 5,
        out_specs=[anywhere] * 4,
        scratch_shapes=[
            pltpu.VMEM((4,) + flat, BF16),
            pltpu.VMEM((4,) + flat, BF16),
            pltpu.VMEM((heads, DH), F32),
            pltpu.VMEM(per_head, BF16),
            pltpu.VMEM((heads, DH, GROUP), BF16),
            pltpu.VMEM(per_head, BF16),
            pltpu.VMEM(per_head, BF16),
            pltpu.VMEM(per_head, F32),
            pltpu.VMEM(per_head, F32),
            pltpu.VMEM(per_head, F32),
            pltpu.VMEM((heads, GROUP, GROUP), BF16),
            pltpu.VMEM(per_head, F32),
            pltpu.VMEM(per_head, BF16),
            pltpu.VMEM(per_head, F32),
            pltpu.VMEM(per_head, F32),
            pltpu.VMEM((heads, DH, DH), BF16),
            pltpu.VMEM((2, heads * DH, DH), F32),
            per_scan(PLANE),
            per_scan(PLANE),
            per_scan(),
            per_scan(levels),
            per_scan(PLANE),
            pltpu.VMEM((2, GROUP, DH), F32),
            dma((5,)),
            dma((2, 2, most)),
            dma((2, 2, most)),
            dma((2, most, levels)),
            dma((2, most, levels)),
            dma((2,)),
            dma((4,)),
            pltpu.SemaphoreType.REGULAR((levels,)),
        ],
        compiler_params=pltpu.CompilerParams(
            collective_id=0, has_side_effects=True, vmem_limit_bytes=60 * 1024 * 1024
        ),
    )(
        query_raw.reshape(flat),
        key_raw.reshape(flat),
        value_raw.reshape(flat),
        out_gain,
        out_grad.reshape(flat),
    )
    outs = pl.pallas_call(
        deliver,
        out_shape=[pltpu.HBM(flat, BF16)] * 4,
        in_specs=[anywhere] * 4,
        out_specs=[in_hbm] * 4,
        scratch_shapes=[dma((4,))],
        compiler_params=pltpu.CompilerParams(vmem_limit_bytes=4 * 1024 * 1024),
    )(*outs)
    return tuple(out.reshape(tokens, heads, width) for out in outs)


def solution(mesh):
    rows = P("seq", "head", None)
    return jax.shard_map(
        body,
        mesh=mesh,
        in_specs=(rows, rows, rows, P("head", None), rows),
        out_specs=(rows,) * 4,
        check_vma=False,
    )
```

```python
import functools

import jax
import jax.numpy as jnp
from jax import lax
from jax.experimental import pallas as pl
from jax.experimental.pallas import tpu as pltpu
from jax.sharding import PartitionSpec as P

GROUP = 256
DH = 128
WIDE, LONG = 4, 8
PLANE = WIDE * LONG
CHUNKS = 2
MESH = pl.DeviceIdType.MESH
F32 = jnp.float32
BF16 = jnp.bfloat16


def dot(lhs, rhs, contract):
    return lax.dot_general(lhs, rhs, (contract, ((), ())), preferred_element_type=F32)


def nn(lhs, rhs):
    return dot(lhs, rhs, ((1,), (0,)))


def nt(lhs, rhs):
    return dot(lhs, rhs, ((1,), (1,)))


def tn(lhs, rhs):
    return dot(lhs, rhs, ((0,), (0,)))


def kernel(
    levels,
    heads,
    cores,
    q_hbm,
    k_hbm,
    v_hbm,
    gain_hbm,
    g_hbm,
    normed_out,
    qg_out,
    kg_out,
    vg_out,
    raw,
    results,
    gain,
    qact,
    qact_t,
    kact,
    vact,
    qslope,
    kslope,
    grad_in,
    attn,
    mixed,
    delta,
    dk,
    dv,
    state_b,
    own,
    gathered,
    prefix,
    total,
    z_slots,
    state,
    stats,
    in_sem,
    send_sem,
    recv_sem,
    z_send_sem,
    z_recv_sem,
    stat_sem,
    out_sem,
    ready,
):
    seq = lax.axis_index("seq")
    core = lax.axis_index("head")
    level = seq // PLANE
    place = lax.rem(seq, PLANE)
    rows = heads * DH // (CHUNKS * PLANE)
    span = heads * DH // CHUNKS
    per = heads // CHUNKS
    width = GROUP // heads

    across, along = place // LONG, lax.rem(place, LONG)

    def each_peer(act):
        half = LONG // 2
        steps = [half]
        for off in range(1, half):
            steps += [half - off, half + off]

        for step in steps + [0]:

            def one(turn, carry, step=step):
                x = lax.rem(across + lax.rem(turn + WIDE // 2, WIDE), WIDE)
                act(x * LONG + lax.rem(along + step, LONG))
                return carry

            if step:
                lax.fori_loop(0, WIDE, one, 0)
            else:
                lax.fori_loop(0, WIDE // 2, one, 0)
                lax.fori_loop(WIDE // 2 + 1, WIDE, one, 0)

    barrier = pltpu.get_barrier_semaphore()

    def greet(peer):
        pl.semaphore_signal(
            barrier, inc=1, device_id=(level * PLANE + peer, core), device_id_type=MESH
        )

    def greet_later(other, carry):
        pl.semaphore_signal(
            barrier, inc=1, device_id=(other * PLANE + place, core), device_id_type=MESH
        )
        return carry

    def answer_earlier(other, carry):
        pl.semaphore_signal(
            ready.at[level], inc=1, device_id=(other * PLANE + place, core), device_id_type=MESH
        )
        return carry

    each_peer(greet)
    loads = [
        pltpu.make_async_copy(hbm, raw.at[i], in_sem.at[i])
        for i, hbm in enumerate((k_hbm, v_hbm, q_hbm, g_hbm))
    ] + [pltpu.make_async_copy(gain_hbm, gain, in_sem.at[4])]
    for load in loads:
        load.start()
    lax.fori_loop(level + 1, levels, greet_later, 0)
    pl.semaphore_signal(barrier, inc=1, device_id=(seq, 1 - core), device_id_type=MESH)

    row = lax.broadcasted_iota(jnp.int32, (GROUP, GROUP), 0)
    col = lax.broadcasted_iota(jnp.int32, (GROUP, GROUP), 1)
    causal = col <= row
    sort = jnp.where(col == lax.rem(row, width) * heads + row // width, 1.0, 0.0).astype(BF16)
    unsort = jnp.where(col == lax.rem(row, heads) * width + row // heads, 1.0, 0.0).astype(BF16)

    def sorted_tiles(i):
        for tile in range(heads):
            yield tile, nn(sort, raw[i, pl.ds(tile * GROUP, GROUP), :])

    def put(dst, tile, value):
        for h in range(heads):
            dst[h, pl.ds(tile * width, width), :] = value[h * width : (h + 1) * width].astype(
                dst.dtype
            )

    def activate(i, act, slope):
        for tile, value in sorted_tiles(i):
            sigma = jax.nn.sigmoid(value)
            put(act, tile, value * sigma)
            put(slope, tile, sigma * (1.0 + value * (1.0 - sigma)))

    def store(i, out, head_value):
        values = [head_value(h).astype(BF16) for h in range(heads)]
        for tile in range(heads):
            piece = jnp.concatenate(
                [value[tile * width : (tile + 1) * width] for value in values], axis=0
            )
            results[i, pl.ds(tile * GROUP, GROUP), :] = nn(unsort, piece).astype(BF16)
        copy = pltpu.make_async_copy(results.at[i], out, out_sem.at[i])
        copy.start()
        return copy

    def bytes_of(ref, sem):
        return pltpu.make_async_copy(ref, ref, sem)

    others = pl.ds(0, PLANE - 1)

    def scatter(scan, chunk):
        def send(peer):
            pltpu.make_async_remote_copy(
                src_ref=own.at[scan, pl.ds(chunk * span + peer * rows, rows), :],
                dst_ref=gathered.at[scan, chunk, place],
                send_sem=send_sem.at[scan, 0, chunk],
                recv_sem=recv_sem.at[scan, 0, chunk],
                device_id=(level * PLANE + peer, core),
                device_id_type=MESH,
            ).start()

        each_peer(send)
        gathered[scan, chunk, place] = own[scan, pl.ds(chunk * span + place * rows, rows), :]

    def wait_scatter(scan, chunk):
        bytes_of(gathered.at[scan, chunk, others], recv_sem.at[scan, 0, chunk]).wait()

    def wait_scatter_send(scan, chunk):
        bytes_of(gathered.at[scan, chunk, others], send_sem.at[scan, 0, chunk]).wait()

    needing = ((level + 1, levels), (0, level))
    needed = ((0, level), (level + 1, levels))

    def z_copy(scan, chunk, target):
        return pltpu.make_async_remote_copy(
            src_ref=total.at[scan, chunk],
            dst_ref=z_slots.at[scan, chunk, level],
            send_sem=z_send_sem.at[scan, chunk, target],
            recv_sem=z_recv_sem.at[scan, chunk, level],
            device_id=(target * PLANE + place, core),
            device_id_type=MESH,
        )

    def own_total(scan, chunk):
        acc = gathered[scan, chunk, 0]
        for p in range(1, PLANE):
            acc = acc + gathered[scan, chunk, p]
        total[scan, chunk] = acc

        def send(target, carry):
            if scan == 0 and chunk == 0:
                pl.semaphore_wait(ready.at[target], 1)
            z_copy(scan, chunk, target).start()
            return carry

        lax.fori_loop(*needing[scan], send, 0)

    def all_prefixes(scan, chunk):
        def take(source, acc):
            bytes_of(z_slots.at[scan, chunk, source], z_recv_sem.at[scan, chunk, source]).wait()
            return acc + z_slots[scan, chunk, source]

        acc = lax.fori_loop(*needed[scan], take, jnp.zeros((rows, DH), F32))
        for p in range(PLANE) if scan == 0 else range(PLANE - 1, -1, -1):
            prefix[scan, chunk, p] = acc
            acc = acc + gathered[scan, chunk, p]

    def give_back(scan, chunk):
        def send(peer):
            pltpu.make_async_remote_copy(
                src_ref=prefix.at[scan, chunk, peer],
                dst_ref=state.at[scan, chunk, place],
                send_sem=send_sem.at[scan, 1, chunk],
                recv_sem=recv_sem.at[scan, 1, chunk],
                device_id=(level * PLANE + peer, core),
                device_id_type=MESH,
            ).start()

        if scan == 0:
            each_peer(send)
        else:

            @pl.when(place != 0)
            def _():
                send(0)

            def unless_first(peer):
                @pl.when(peer != 0)
                def _():
                    send(peer)

            each_peer(unless_first)
        state[scan, chunk, place] = prefix[scan, chunk, place]

    def wait_back(scan, chunk):
        bytes_of(state.at[scan, chunk, others], recv_sem.at[scan, 1, chunk]).wait()

    def drain(scan):
        for chunk in range(CHUNKS):
            wait_scatter_send(scan, chunk)
            bytes_of(state.at[scan, chunk, others], send_sem.at[scan, 1, chunk]).wait()

            def sent(target, carry):
                z_copy(scan, chunk, target).wait_send()
                return carry

            lax.fori_loop(*needing[scan], sent, 0)

    def middle(scan, work):
        for chunk in range(CHUNKS):
            wait_scatter(scan, chunk)
            own_total(scan, chunk)
        work()
        for chunk in range(CHUNKS):
            all_prefixes(scan, chunk)
            give_back(scan, chunk)

    def scanned(scan, h):
        chunk, at = h // per, h % per
        parts = PLANE // per
        return state[scan, chunk, pl.ds(at * parts, parts)].reshape(DH, DH).astype(BF16)

    loads[0].wait()
    activate(0, kact, kslope)
    loads[1].wait()
    for tile, value in sorted_tiles(1):
        put(vact, tile, value)
    for h in range(heads):
        own[0, pl.ds(h * DH, DH), :] = tn(kact[h], vact[h])

    pl.semaphore_wait(barrier, PLANE + level)
    lax.fori_loop(0, level, answer_earlier, 0)
    for chunk in range(CHUNKS):
        scatter(0, chunk)

    loads[2].wait()
    activate(2, qact, qslope)
    for h in range(heads):
        qact_t[h] = qact[h].T
        scores = nt(qact[h], kact[h])
        attn[h] = jnp.where(causal, scores, 0.0).astype(BF16)
        mixed[h] = nn(attn[h], vact[h])

    def weigh_grad():
        loads[3].wait()
        loads[4].wait()
        for tile, value in sorted_tiles(3):
            for h in range(heads):
                grad_in[h, pl.ds(tile * width, width), :] = (
                    value[h * width : (h + 1) * width] * gain[pl.ds(h, 1), :]
                )

    weigh_grad()
    middle(0, lambda: None)

    square = jnp.zeros((GROUP, DH), F32)
    crossed = jnp.zeros((GROUP, DH), F32)
    for h in range(heads):
        if h % per == 0:
            wait_back(0, h // per)
        state_b[h] = scanned(0, h)
        value = mixed[h] + nn(qact[h], state_b[h])
        mixed[h] = value
        square = square + value * value
        crossed = crossed + grad_in[h] * value
    square = jnp.sum(square, axis=1, keepdims=True)
    crossed = jnp.sum(crossed, axis=1, keepdims=True)
    lane = lax.broadcasted_iota(jnp.int32, (GROUP, DH), 1)
    stats[0] = jnp.where(lane == 0, square, jnp.where(lane == 1, crossed, 0.0))
    exchange = pltpu.make_async_remote_copy(
        src_ref=stats.at[0],
        dst_ref=stats.at[1],
        send_sem=stat_sem.at[0],
        recv_sem=stat_sem.at[1],
        device_id=(seq, 1 - core),
        device_id_type=MESH,
    )
    exchange.start()
    exchange.wait_recv()
    both = stats[1]
    features = heads * cores * DH
    square = square + both[:, 0:1]
    crossed = crossed + both[:, 1:2]
    inv_rms = lax.rsqrt(square * (1.0 / features) + 1e-06)
    factor = crossed * (inv_rms * inv_rms * inv_rms) * (1.0 / features)
    for h in range(heads):
        delta[h] = (grad_in[h] * inv_rms - mixed[h] * factor).astype(BF16)
        own[1, pl.ds(h * DH, DH), :] = nn(qact_t[h], delta[h])
        if (h + 1) % per == 0:
            scatter(1, h // per)

    copies = [store(0, normed_out, lambda h: mixed[h] * inv_rms * gain[pl.ds(h, 1), :])]

    def local_grads(some_heads):
        for h in some_heads:
            bscore = jnp.where(causal, nt(delta[h], vact[h]), 0.0).astype(BF16)
            mixed[h] = (nn(bscore, kact[h]) + nt(delta[h], state_b[h])) * qslope[h]
            dk[h] = tn(bscore, qact[h])
            dv[h] = tn(attn[h], delta[h])

    local_grads(range(heads // 2))
    middle(1, lambda: None)
    local_grads(range(heads // 2, heads))
    copies.append(store(1, qg_out, lambda h: mixed[h]))
    exchange.wait_send()
    drain(0)

    for h in range(heads):
        if h % per == 0:
            wait_back(1, h // per)
        state_b[h] = scanned(1, h)
        dk[h] = (dk[h] + nt(vact[h], state_b[h])) * kslope[h]
        dv[h] = dv[h] + nn(kact[h], state_b[h])
    copies.append(store(2, kg_out, lambda h: dk[h]))
    copies.append(store(3, vg_out, lambda h: dv[h]))
    drain(1)
    for copy in copies:
        copy.wait()


def deliver(*refs):
    count = len(refs) // 2
    sems = refs[-1]
    copies = [
        pltpu.make_async_copy(refs[i], refs[count + i], sems.at[i]) for i in range(count)
    ]
    for copy in copies:
        copy.start()
    for copy in copies:
        copy.wait()


def body(query_raw, key_raw, value_raw, out_gain, out_grad):
    tokens, heads, width = query_raw.shape
    levels = lax.axis_size("seq") // PLANE
    cores = lax.axis_size("head")
    flat = (tokens * heads, width)
    rows = heads * DH // (CHUNKS * PLANE)
    anywhere = pl.BlockSpec(memory_space=pl.ANY)
    in_hbm = pl.BlockSpec(memory_space=pltpu.HBM)
    per_head = (heads, GROUP, DH)
    dma = pltpu.SemaphoreType.DMA
    outs = pl.pallas_call(
        functools.partial(kernel, levels, heads, cores),
        out_shape=[pltpu.VMEM(flat, BF16)] * 4,
        in_specs=[in_hbm] * 5,
        out_specs=[anywhere] * 4,
        scratch_shapes=[
            pltpu.VMEM((4,) + flat, BF16),
            pltpu.VMEM((4,) + flat, BF16),
            pltpu.VMEM((heads, DH), F32),
            pltpu.VMEM(per_head, BF16),
            pltpu.VMEM((heads, DH, GROUP), BF16),
            pltpu.VMEM(per_head, BF16),
            pltpu.VMEM(per_head, BF16),
            pltpu.VMEM(per_head, F32),
            pltpu.VMEM(per_head, F32),
            pltpu.VMEM(per_head, F32),
            pltpu.VMEM((heads, GROUP, GROUP), BF16),
            pltpu.VMEM(per_head, F32),
            pltpu.VMEM(per_head, BF16),
            pltpu.VMEM(per_head, F32),
            pltpu.VMEM(per_head, F32),
            pltpu.VMEM((heads, DH, DH), BF16),
            pltpu.VMEM((2, heads * DH, DH), F32),
            pltpu.VMEM((2, CHUNKS, PLANE, rows, DH), F32),
            pltpu.VMEM((2, CHUNKS, PLANE, rows, DH), F32),
            pltpu.VMEM((2, CHUNKS, rows, DH), F32),
            pltpu.VMEM((2, CHUNKS, levels, rows, DH), F32),
            pltpu.VMEM((2, CHUNKS, PLANE, rows, DH), F32),
            pltpu.VMEM((2, GROUP, DH), F32),
            dma((5,)),
            dma((2, 2, CHUNKS)),
            dma((2, 2, CHUNKS)),
            dma((2, CHUNKS, levels)),
            dma((2, CHUNKS, levels)),
            dma((2,)),
            dma((4,)),
            pltpu.SemaphoreType.REGULAR((levels,)),
        ],
        compiler_params=pltpu.CompilerParams(
            collective_id=0, has_side_effects=True, vmem_limit_bytes=60 * 1024 * 1024
        ),
    )(
        query_raw.reshape(flat),
        key_raw.reshape(flat),
        value_raw.reshape(flat),
        out_gain,
        out_grad.reshape(flat),
    )
    outs = pl.pallas_call(
        deliver,
        out_shape=[pltpu.HBM(flat, BF16)] * 4,
        in_specs=[anywhere] * 4,
        out_specs=[in_hbm] * 4,
        scratch_shapes=[dma((4,))],
        compiler_params=pltpu.CompilerParams(vmem_limit_bytes=4 * 1024 * 1024),
    )(*outs)
    return tuple(out.reshape(tokens, heads, width) for out in outs)


def solution(mesh):
    rows = P("seq", "head", None)
    return jax.shard_map(
        body,
        mesh=mesh,
        in_specs=(rows, rows, rows, P("head", None), rows),
        out_specs=(rows,) * 4,
        check_vma=False,
    )
```
